256 devices in a mesh: wide: 64 (over z, x, core), layer: 4 (over y).
Axes of the slice: x: 4, y: 4, z: 8, core: 2. Of those that a mesh axis runs over, the one named last changes fastest.
Arguments:
- members: bfloat16 [384, 8, 32768], P('wide', 'layer'), may hold values from -6 to 6
- courant: float32 [8, 32768], P('layer'), may hold values from 0.2 to 0.9
- obs_value: float32 [2, 8, 256, 128], replicated, may hold values from -8 to 8
- obs_rinv: float32 [8, 256, 128], replicated, may hold values from 0.5 to 8
- obs_cell: int32 [8, 256, 128], replicated, may hold values from 0 to 127
- obs_count: int32 [8, 256], replicated, may hold values from 1 to 128, as said below
Outputs:
- analysis: bfloat16 [384, 8, 32768], P('wide', 'layer')
The draws below stay inside these ranges and needn't reach their ends.
Inputs may be any that keep to these rules, and one draw needn't show every extreme that they name: `obs_count`: slots 0 to count - 1 of a level and region are live; in every draw some level and region has all 128 slots live.
All inputs are finite; a program needn't handle non-finite values.
Results may differ from the reference program's by a relative error of at most 0.0079.
The reference program's roundings to bfloat16 on the way count: a program that leaves them out, or rounds other values in their place, can miss the bound.
Values may be sent and summed in bfloat16 or wider, within the bound.
A program may use at most 64 MiB of HBM per device.

```python
import math
import jax
import jax.numpy as jnp
from jax import lax

K = 384
NLEV = 8
RCELLS = 128
OBS_LEV = 128
ITERS = 5
ADV = 2
CYCLES = 2
REGIONS = 256
CELLS = 32768


def draw_obs_count(key, part):
    first, second, third = jax.random.split(jax.random.fold_in(key, 17), 3)
    lower = jax.random.randint(first, (NLEV, REGIONS), 1, OBS_LEV + 1)
    upper = jax.random.randint(second, (NLEV, REGIONS), 1, OBS_LEV + 1)
    counts = jnp.minimum(lower, upper).reshape(-1)
    chosen = jax.random.randint(third, (), 0, NLEV * REGIONS)
    counts = jnp.where(jnp.arange(NLEV * REGIONS) == chosen, OBS_LEV, counts)
    return counts.reshape(NLEV, REGIONS).astype(jnp.int32)


def touch_ends(array, stream_key, smallest, high):
    longest = array.shape.index(max(array.shape))
    spots = []
    for shift in (0, 1):
        where = [jax.random.randint(jax.random.fold_in(stream_key, axis), (), 0, length) for axis, length in enumerate(array.shape)]
        where[longest] = (where[longest] + shift) % array.shape[longest]
        spots.append(tuple(where))
    return array.at[spots[0]].set(smallest).at[spots[1]].set(high)


def shard_levels(rng, extent, shards, least, top_value):
    factor_of, own = 1.0, jax.random.fold_in(rng, 6)
    for position, shards_of in shards:
        draws = jnp.exp(jax.random.uniform(jax.random.fold_in(own, position), (shards_of,), jnp.float32, least / len(shards), top_value / len(shards)))
        factor_of = factor_of * jnp.repeat(draws, extent[position] // shards_of).reshape([-1 if axis == position else 1 for axis in range(len(extent))])
    return factor_of


def bell_draw(rng, shape, scale, bound, cuts=(), held_as=jnp.bfloat16):
    drawn = scale * jax.random.normal(rng, shape, jnp.float32)
    if cuts:
        drawn = drawn * shard_levels(rng, shape, cuts, -0.22, 0.18)
    return jnp.clip(drawn, -bound, bound).astype(held_as)


def setup_inputs(seed: int = 0) -> dict:
    key_list = jax.random.split(jax.random.key(seed), 7)
    return {
        "members": bell_draw(key_list[0], (K, NLEV, CELLS), 1.0, 6.0, ((0, 64), (1, 4))),
        "courant": jnp.clip(0.2 + 0.7 * jax.random.uniform(key_list[1], (NLEV, CELLS), jnp.float32) ** shard_levels(key_list[1], (NLEV, CELLS), ((0, 4),), -0.2, 0.2), 0.2, 0.9),
        "obs_value": bell_draw(key_list[2], (CYCLES, NLEV, REGIONS, OBS_LEV), 1.5, 8.0, (), jnp.float32),
        "obs_rinv": jnp.clip(jnp.exp(jax.random.uniform(key_list[3], (NLEV, REGIONS, OBS_LEV), jnp.float32, math.log(0.5), math.log(8.0))), 0.5, 8.0),
        "obs_cell": touch_ends(jax.random.randint(key_list[4], (NLEV, REGIONS, OBS_LEV), 0, RCELLS), jax.random.fold_in(key_list[4], 1), 0, RCELLS - 1).astype(jnp.int32),
        "obs_count": draw_obs_count(jax.random.fold_in(key_list[6], 71), 0),
    }


def advect(field, courant):
    for step in range(ADV):
        field = field - courant * (field - jnp.roll(field, 1, axis=2))
    return field

def weigh(yrows, cells, rinv, counts, values):
    members = yrows.shape[0]
    slots = cells.shape[2]
    side = (jnp.arange(3, dtype=jnp.int32) - 1)[None, :, None]
    offset = (side * RCELLS + cells).astype(jnp.float32) - 0.5 * (RCELLS - 1)
    ratio = offset / RCELLS
    local = jnp.exp(-(ratio * ratio))
    slot_ids = jnp.arange(slots, dtype=jnp.int32)[None, None, :]
    live = (slot_ids < counts[:, :, None]).astype(jnp.int32)
    weight = rinv * local * live.astype(jnp.float32)
    ensemble = yrows.astype(jnp.float32)
    ybar = lax.optimization_barrier(jnp.mean(ensemble, axis=0))
    anomaly = ensemble - ybar
    innov = values - ybar
    scaled = (anomaly * jnp.sqrt(weight)).astype(jnp.bfloat16).reshape(members, -1)
    vector = lax.optimization_barrier(jnp.sum((anomaly * (weight * innov)).reshape(members, -1), axis=1))
    return (scaled, vector, live.reshape(-1))

def transform(gram, vector):
    size = gram.shape[0]
    eye = jnp.eye(size, dtype=jnp.float32)
    amat = (size - 1.0) * eye + gram
    scale = jnp.sqrt(jnp.sum(amat * amat))
    iterate = amat / scale
    inverse = eye
    for step in range(ITERS):
        middle = 1.5 * eye - 0.5 * jnp.dot(inverse, iterate, precision=lax.Precision.HIGHEST)
        iterate = jnp.dot(iterate, middle, precision=lax.Precision.HIGHEST)
        inverse = jnp.dot(middle, inverse, precision=lax.Precision.HIGHEST)
    cov = jnp.dot(inverse, inverse, precision=lax.Precision.HIGHEST) / scale
    wmat = jnp.sqrt((size - 1.0) / scale) * inverse
    wbar = jnp.dot(cov, vector[:, None], precision=lax.Precision.HIGHEST)[:, 0]
    return wmat + wbar[:, None]

def update(slab, trans):
    ensemble = slab.astype(jnp.float32)
    mean = lax.optimization_barrier(jnp.mean(ensemble, axis=0))
    anomaly = ensemble - mean
    moved = jnp.einsum('jk,jlc->klc', trans, anomaly, precision=lax.Precision.HIGHEST)
    return (mean + moved).astype(jnp.bfloat16)

def analyse(state, values, rinv, cells, counts):
    members, levels, total = state.shape
    regions = cells.shape[1]

    def one(region):
        ids = (region - 1 + jnp.arange(3, dtype=jnp.int32)) % regions
        near_cells = jnp.take(cells, ids, axis=1)
        slabs = []
        rows = []
        for i in range(3):
            start = (ids[i] * RCELLS).astype(jnp.int32)
            slab = lax.dynamic_slice_in_dim(state, start, RCELLS, 2)
            index = jnp.broadcast_to(near_cells[None, :, i, :], (members, levels, near_cells.shape[2]))
            slabs.append(slab)
            rows.append(jnp.take_along_axis(slab, index, axis=2))
        yrows = jnp.stack(rows, axis=2)
        scaled, vector, live = weigh(yrows, near_cells, jnp.take(rinv, ids, axis=1), jnp.take(counts, ids, axis=1), jnp.take(values, ids, axis=1))
        wide_rows = scaled.astype(jnp.float32)
        gram = jnp.dot(wide_rows, wide_rows.T, precision=lax.Precision.HIGHEST)
        return update(slabs[1], transform(gram, vector))
    result = lax.map(one, jnp.arange(regions, dtype=jnp.int32))
    return result.transpose(1, 2, 0, 3).reshape(members, levels, total)

def reference(members, courant, obs_value, obs_rinv, obs_cell, obs_count):
    state = members
    for cycle in range(CYCLES):
        state = advect(state.astype(jnp.float32), courant).astype(jnp.bfloat16)
        state = analyse(state, obs_value[cycle], obs_rinv, obs_cell, obs_count)
    return state
```

```python
import functools

import jax
import jax.numpy as jnp
from jax import lax
from jax.experimental import pallas as pl
from jax.experimental.pallas import tpu as pltpu
from jax.sharding import PartitionSpec as P

K = 384
LEV = 8
RC = 128
ITERS = 5
CYCLES = 2
F32, BF16 = jnp.float32, jnp.bfloat16
MESH = pl.DeviceIdType.MESH
PAIRS = ((0, 0), (0, 1), (0, 2), (1, 1), (1, 2), (2, 2))


def region_of(w, y):
    return 4 * w + y


def device_of(r):
    return r // 4, r % 4


def dot(a, b):
    return jnp.dot(a, b, preferred_element_type=F32)


def halves(a):
    high = a.astype(BF16)
    return high, (a - high.astype(F32)).astype(BF16)


def dot3(a, b):
    (ah, al), (bh, bl) = a, b
    return dot(ah, bh) + dot(ah, bl) + dot(al, bh)


def iota(shape, dim):
    return lax.broadcasted_iota(jnp.int32, shape, dim)


def cycles_kernel(
    st_ref, cour_ref, val_ref, rinv_ref, cell_ref, count_ref, o_ref,
    fc, sc, acc, gram, tz, xbar, hs, hr, gs, gr, vs, vr, hsem, gsem, vsem,
):
    me = region_of(lax.axis_index("wide"), lax.axis_index("layer"))
    left, right = device_of((me + 255) % 256), device_of((me + 1) % 256)
    barrier = pltpu.get_barrier_semaphore()
    for side in (left, right):
        pl.semaphore_signal(barrier, inc=1, device_id=side, device_id_type=MESH)
    pl.semaphore_wait(barrier, 2)
    o_ref[...] = st_ref[...]
    lane = iota((K, RC), 1)
    last = lane == RC - 1

    def shifted(u, before):
        return pltpu.roll(jnp.where(last, before, u), 1, axis=1)

    def cycle(c, carry):
        def edge(l, total):
            src, dst = iota((RC, RC), 0), iota((RC, RC), 1)
            pick = (src - (RC - 2) == dst - 2 * l) & (src >= RC - 2)
            return total + dot(o_ref[l], pick.astype(F32).astype(BF16))

        hs[c] = lax.fori_loop(0, LEV, edge, jnp.zeros((K, RC), F32)).astype(BF16)
        halo = pltpu.make_async_remote_copy(
            hs.at[c], hr.at[c], hsem.at[0, c], hsem.at[1, c], device_id=right, device_id_type=MESH
        )
        halo.start()
        halo.wait()
        acc[...] = jnp.zeros_like(acc)

        def level(l, carry):
            col = pl.ds(pl.multiple_of(l * RC, RC), RC)
            own = cour_ref[l, :, RC:]
            prior = cour_ref[l, :, :RC]
            before = pltpu.roll(hr[c].astype(F32), RC - 2 - 2 * l, axis=1)
            u = o_ref[l].astype(F32)
            u1 = u - own * (u - shifted(u, before))
            before1 = before - prior * (before - pltpu.roll(before, 1, axis=1))
            f = (u1 - own * (u1 - shifted(u1, before1))).astype(BF16)
            fc[l] = f
            cells = cell_ref[l]
            pick = (iota((RC, RC), 0) == cells).astype(F32).astype(BF16)
            ens = dot(f, pick)
            ybar = jnp.sum(ens, axis=0, keepdims=True) * (1.0 / K)
            anom = ens - ybar
            innov = val_ref[c, l] - ybar
            live = (iota((1, RC), 1) < count_ref[l]).astype(F32)
            for i in range(3):
                ratio = ((i - 1) * RC + cells).astype(F32) * (1.0 / RC) - (0.5 * (RC - 1)) / RC
                weight = rinv_ref[l] * jnp.exp(-(ratio * ratio)) * live
                sc[i, :, col] = (anom * jnp.sqrt(weight)).astype(BF16)
                acc[i] += anom * (weight * innov)
            return carry

        lax.fori_loop(0, LEV, level, 0)

        def gram_of(i):
            return lax.dot_general(
                sc[i], sc[i], (((1,), (1,)), ((), ())), preferred_element_type=F32
            )

        def vec_of(i):
            return jnp.sum(acc[i].T, axis=0, keepdims=True)

        sent = []
        for side, i, to in ((0, 2, left), (1, 0, right)):
            gram[...] = gram_of(i)
            for b, (p, q) in enumerate(PAIRS):
                gs[c, side, b] = gram[p * 128 : p * 128 + 128, q * 128 : q * 128 + 128]
            vs[c, side] = jnp.broadcast_to(vec_of(i), (8, K))
            for k, (src, dst, sem) in enumerate(((gs, gr, gsem), (vs, vr, vsem))):
                copy = pltpu.make_async_remote_copy(
                    src.at[c, side], dst.at[c, side], sem.at[0, c, side], sem.at[1, c, side],
                    device_id=to, device_id_type=MESH,
                )
                copy.start()
                sent.append(copy)
        gram[...] = gram_of(1)
        vec = vec_of(1)

        def parts(l, carry):
            col = pl.ds(pl.multiple_of(l * RC, RC), RC)
            f = fc[l].astype(F32)
            mean = jnp.sum(f, axis=0, keepdims=True) * (1.0 / K)
            xbar[:, col] = jnp.broadcast_to(mean, (8, RC))
            sc[0, :, col], sc[1, :, col] = halves(f - mean)
            return carry

        for copy in sent:
            copy.wait()
        lax.fori_loop(0, LEV, parts, 0)
        vec = vec + vr[c, 0, 0:1] + vr[c, 1, 0:1]
        for b, (p, q) in enumerate(PAIRS):
            block = gram[p * 128 : p * 128 + 128, q * 128 : q * 128 + 128] + gr[c, 0, b] + gr[c, 1, b]
            gram[p * 128 : p * 128 + 128, q * 128 : q * 128 + 128] = block
            if p != q:
                gram[q * 128 : q * 128 + 128, p * 128 : p * 128 + 128] = block.T
        eye = iota((K, K), 0) == iota((K, K), 1)
        amat = gram[...] + jnp.where(eye, K - 1.0, 0.0)
        scale = jnp.sqrt(jnp.sum(jnp.sum(amat * amat, axis=0, keepdims=True), axis=1, keepdims=True))
        first = amat / scale

        def advance(t):
            high, low = halves(t)
            square = dot3((high, low), (high, low))
            return 2.25 * t + dot3(halves(square), halves(0.25 * t - jnp.where(eye, 1.5, 0.0)))

        tz[1] = jnp.where(eye, 1.5, 0.0) - 0.5 * first
        tz[0] = advance(first)

        def newton(i, carry):
            t, z = tz[0], tz[1]
            tz[1] = 1.5 * z - 0.5 * dot3(halves(t), halves(z))
            tz[0] = advance(t)
            return carry

        lax.fori_loop(0, ITERS - 2, newton, 0)
        z = 1.5 * tz[1] - 0.5 * dot3(halves(tz[0]), halves(tz[1]))
        half = jnp.sum(z * vec, axis=1, keepdims=True)
        wbar = jnp.sum(z * half, axis=0, keepdims=True) / scale
        wh, wl = halves(jnp.sqrt((K - 1.0) / scale) * z + wbar)
        for j in range(LEV // 2):
            cols = slice(256 * j, 256 * j + 256)
            new = dot3((wh, wl), (sc[0, :, cols], sc[1, :, cols])) + xbar[0:1, cols]
            o_ref[2 * j] = new[:, :RC].astype(BF16)
            o_ref[2 * j + 1] = new[:, RC:].astype(BF16)
        return carry

    lax.fori_loop(0, CYCLES, cycle, 0)


def run_cycles(state, cour, values, rinv, cells, counts):
    vmem = pl.BlockSpec(memory_space=pltpu.VMEM)
    return pl.pallas_call(
        cycles_kernel,
        out_shape=jax.ShapeDtypeStruct((LEV, K, RC), BF16),
        in_specs=[vmem] * 6,
        out_specs=vmem,
        scratch_shapes=[
            pltpu.VMEM((LEV, K, RC), BF16),
            pltpu.VMEM((3, K, LEV * RC), BF16),
            pltpu.VMEM((3, K, RC), F32),
            pltpu.VMEM((K, K), F32),
            pltpu.VMEM((2, K, K), F32),
            pltpu.VMEM((8, LEV * RC), F32),
            pltpu.VMEM((CYCLES, K, RC), BF16),
            pltpu.VMEM((CYCLES, K, RC), BF16),
            pltpu.VMEM((CYCLES, 2, 6, 128, 128), F32),
            pltpu.VMEM((CYCLES, 2, 6, 128, 128), F32),
            pltpu.VMEM((CYCLES, 2, 8, K), F32),
            pltpu.VMEM((CYCLES, 2, 8, K), F32),
            pltpu.SemaphoreType.DMA((2, CYCLES)),
            pltpu.SemaphoreType.DMA((2, CYCLES, 2)),
            pltpu.SemaphoreType.DMA((2, CYCLES, 2)),
        ],
        compiler_params=pltpu.CompilerParams(
            collective_id=1, has_side_effects=True, vmem_limit_bytes=56 * 2**20
        ),
    )(state, cour, values, rinv, cells, counts)


def courant_here(courant):
    w = lax.axis_index("wide")
    extended = jnp.concatenate([courant[:, -RC:], courant], axis=1)
    near = lax.dynamic_slice_in_dim(extended, w * 4 * RC, 5 * RC, 1)
    blocks = jnp.stack([near[:, i * RC : i * RC + 2 * RC] for i in range(4)])
    return lax.all_to_all(blocks, "layer", 0, 0, tiled=True).reshape(LEV, 1, 2 * RC)


def per_device(members, courant, obs_value, obs_rinv, obs_cell, obs_count):
    region = region_of(lax.axis_index("wide"), lax.axis_index("layer"))

    def here(table, axis):
        return lax.dynamic_slice_in_dim(table, region, 1, axis)

    cour = courant_here(courant)
    counts = jnp.broadcast_to(here(obs_count, 1)[:, None], (LEV, 1, RC))
    blocks = members.reshape(6, 2, 256, RC).transpose(2, 0, 1, 3)
    blocks = lax.all_to_all(blocks, ("wide", "layer"), 0, 0, tiled=True)
    state = blocks.reshape(64, 4, 6, 2, RC).transpose(1, 3, 0, 2, 4).reshape(LEV, K, RC)
    state = run_cycles(
        state, cour, here(obs_value, 2), here(obs_rinv, 1), here(obs_cell, 1), counts
    )
    blocks = state.reshape(4, 2, 64, 6, RC).transpose(2, 0, 3, 1, 4).reshape(256, 6, 2, RC)
    blocks = lax.all_to_all(blocks, ("wide", "layer"), 0, 0, tiled=True)
    return blocks.transpose(1, 2, 0, 3).reshape(6, 2, 256 * RC)


def solution(mesh):
    placed = (P("wide", "layer", None), P("layer", None), P(), P(), P(), P())
    return jax.shard_map(
        per_device, mesh=mesh, in_specs=placed, out_specs=P("wide", "layer", None), check_vma=False
    )
```

```python
import functools

import jax
import jax.numpy as jnp
from jax import lax
from jax.experimental import pallas as pl
from jax.experimental.pallas import tpu as pltpu
from jax.sharding import PartitionSpec as P

K = 384
LEV = 8
RC = 128
ITERS = 5
CYCLES = 2
F32, BF16 = jnp.float32, jnp.bfloat16
MESH = pl.DeviceIdType.MESH
CHUNKS = 2
PART = 6 // CHUNKS
PLANE = 32 * RC
PAIRS = ((0, 0), (0, 1), (0, 2), (1, 1), (1, 2), (2, 2))


def order_in_plane(z, q, y):
    a = (y + z) % 4
    return a * 8 + ((q // 2 + a) % 4) * 2 + q % 2


def device_of(r):
    z, a, b, core = r // 32, (r // 8) % 4, (r // 2) % 4, r % 2
    return z * 8 + ((b - a + 4) % 4) * 2 + core, (a - z + 8) % 4


def dot(a, b):
    return jnp.dot(a, b, preferred_element_type=F32)


def halves(a):
    high = a.astype(BF16)
    return high, (a - high.astype(F32)).astype(BF16)


def dot3(a, b):
    (ah, al), (bh, bl) = a, b
    return dot(ah, bh) + dot(ah, bl) + dot(al, bh)


def iota(shape, dim):
    return lax.broadcasted_iota(jnp.int32, shape, dim)


def whole_kernel(
    mem_ref, cour_ref, val_ref, rinv_ref, cell_ref, count_ref, o_ref,
    b1, land, leave, b2, st, near, tabv, tabr, tabc, tabn, vals, cells, roots, weights,
    fc, sc, acc, gram, tz, xbar, hs, hr, gs, gr, vs, vr,
    zin, pin, pout, zout, csem, tsem, lsem, hsem, gsem, vsem,
):
    w, y = lax.axis_index("wide"), lax.axis_index("layer")
    z, q = w // 8, w % 8
    here = order_in_plane(z, q, y)
    me = z * 32 + here
    mine = y * 8 + q
    left, right = device_of((me + 255) % 256), device_of((me + 1) % 256)

    def z_partner(s):
        z2 = (z + s) % 8
        return z2, (z2 * 8 + q, y)

    def plane_partner(s):
        q2, y2 = (q + s) % 8, (y + s // 8) % 4
        return q2, y2, (z * 8 + q2, y2)

    def cells_of(r, n=RC):
        return pl.ds(pl.multiple_of(r * RC, RC), n)

    def remote(src, dst, sems, to):
        return pltpu.make_async_remote_copy(
            src, dst, sems.at[0], sems.at[1], device_id=to, device_id_type=MESH
        )

    def drain(ref, sem):
        pltpu.make_async_copy(ref, ref, sem).wait()

    def local(src, dst, k):
        return pltpu.make_async_copy(src, dst, lsem.at[k])

    barrier = pltpu.get_barrier_semaphore()

    def greet(device):
        pl.semaphore_signal(barrier, inc=1, device_id=device, device_id_type=MESH)

    def greet_plane(s, carry):
        greet(plane_partner(s)[2])
        return carry

    def greet_z(s, carry):
        greet(z_partner(s)[1])
        return carry

    lax.fori_loop(1, 8, greet_z, 0)
    lax.fori_loop(1, 32, greet_plane, 0)
    greet(left)
    greet(right)
    row8 = pl.ds(pl.multiple_of(me // 8 * 8, 8), 8)
    tables = [
        pltpu.make_async_copy(val_ref.at[:, :, row8], tabv, tsem.at[0]),
        pltpu.make_async_copy(rinv_ref.at[:, row8], tabr, tsem.at[1]),
        pltpu.make_async_copy(cell_ref.at[:, row8], tabc, tsem.at[2]),
        pltpu.make_async_copy(count_ref, tabn, tsem.at[3]),
    ]
    for copy in tables:
        copy.start()
    own_plane = cells_of(z * 32, PLANE)
    keep = local(mem_ref.at[:, :, own_plane], b1.at[z], 0)
    keep.start()
    pl.semaphore_wait(barrier, 40)

    for ch in range(CHUNKS):
        some = pl.ds(ch * PART, PART)

        def send_z(s, carry, some=some, ch=ch):
            z2, to = z_partner(s)
            src = mem_ref.at[some, :, cells_of(z2 * 32, PLANE)]
            remote(src, b1.at[z, some], zin.at[ch], to).start()
            return carry

        lax.fori_loop(1, 8, send_z, 0)

    before_me = (me + 255) % 256
    keeps = [local(cour_ref.at[:, :, cells_of(me)], near.at[0, pl.ds(2 * y, 2)], 1),
             local(cour_ref.at[:, :, cells_of(before_me)], near.at[1, pl.ds(2 * y, 2)], 2)]
    for copy in keeps:
        copy.start()

    def send_courant(s, carry):
        y2 = (y + s) % 4
        r = z * 32 + order_in_plane(z, q, y2)
        for k, r2 in enumerate((r, (r + 255) % 256)):
            dst = near.at[k, pl.ds(2 * y, 2)]
            remote(cour_ref.at[:, :, cells_of(r2)], dst, csem.at[k], (w, y2)).start()
        return carry

    lax.fori_loop(1, 4, send_courant, 0)

    for copy in tables:
        copy.wait()
    mine8 = me % 8
    at8 = iota((8, RC), 0) == mine8
    count = jnp.sum(jnp.where(iota((LEV, 256), 1) == me, tabn[...], 0), axis=1, keepdims=True)
    live = (iota((LEV, RC), 1) < count).astype(F32)
    for l in range(LEV):
        for c in range(CYCLES):
            vals[c, l] = jnp.sum(jnp.where(at8, tabv[c, l], 0.0), axis=0, keepdims=True)
        cell = jnp.sum(jnp.where(at8, tabc[l], 0), axis=0, keepdims=True)
        cells[l] = cell
        rinv = jnp.sum(jnp.where(at8, tabr[l], 0.0), axis=0, keepdims=True)
        for i in range(3):
            ratio = (((i - 1) * RC + cell).astype(F32) - 0.5 * (RC - 1)) * (1.0 / RC)
            weight = rinv * jnp.exp(-(ratio * ratio)) * live[l : l + 1]
            weights[i, l] = weight
            roots[i, l] = jnp.sqrt(weight)
    keep.wait()

    for ch in range(CHUNKS):
        some = pl.ds(ch * PART, PART)
        drain(b1.at[pl.ds(0, 7), some], zin.at[ch, 1])

        def send_plane(s, carry, some=some, ch=ch):
            q2, y2, to = plane_partner(s)
            src = b1.at[:, some, :, cells_of(order_in_plane(z, q2, y2))]
            remote(src, land.at[mine, :, some], pin.at[ch], to).start()
            return carry

        lax.fori_loop(1, 32, send_plane, 0)
    keep = local(b1.at[:, :, :, cells_of(here)], land.at[mine], 0)
    keep.start()
    for copy in keeps:
        copy.wait()
    for k in range(2):
        drain(near.at[k, pl.ds(0, 6)], csem.at[k, 1])
    keep.wait()
    for ch in range(CHUNKS):
        drain(land.at[pl.ds(0, 31), :, pl.ds(ch * PART, PART)], pin.at[ch, 1])

    out, col = iota((256, 256), 0), iota((256, 256), 1)
    apart = (col == (out % 128) * 2 + out // 128).astype(F32).astype(BF16)
    together = (out == (col % 128) * 2 + col // 128).astype(F32).astype(BF16)

    def unpack(v, carry):
        rows = land[pl.ds(v * 8, 8)].reshape(2 * K, RC)
        for b in range(3):
            both = dot(apart, rows[256 * b : 256 * b + 256]).astype(BF16)
            st[2 * v, 128 * b : 128 * b + 128] = both[:128]
            st[2 * v + 1, 128 * b : 128 * b + 128] = both[128:]
        return carry

    lax.fori_loop(0, 4, unpack, 0)
    lane = iota((K, RC), 1)
    last = lane == RC - 1

    def shifted(u, before):
        return pltpu.roll(jnp.where(last, before, u), 1, axis=1)

    def cycle(c, carry):
        def edge(l, total):
            src, dst = iota((RC, RC), 0), iota((RC, RC), 1)
            pick = (src - (RC - 2) == dst - 2 * l) & (src >= RC - 2)
            return total + dot(st[l], pick.astype(F32).astype(BF16))

        hs[c] = lax.fori_loop(0, LEV, edge, jnp.zeros((K, RC), F32)).astype(BF16)
        halo = pltpu.make_async_remote_copy(
            hs.at[c], hr.at[c], hsem.at[0, c], hsem.at[1, c], device_id=right, device_id_type=MESH
        )
        halo.start()
        halo.wait()
        acc[...] = jnp.zeros_like(acc)

        def level(l, carry):
            col = pl.ds(pl.multiple_of(l * RC, RC), RC)
            own = near[0, l]
            prior = near[1, l]
            before = pltpu.roll(hr[c].astype(F32), RC - 2 - 2 * l, axis=1)
            u = st[l].astype(F32)
            u1 = u - own * (u - shifted(u, before))
            before1 = before - prior * (before - pltpu.roll(before, 1, axis=1))
            f = (u1 - own * (u1 - shifted(u1, before1))).astype(BF16)
            fc[l] = f
            pick = (iota((RC, RC), 0) == cells[l]).astype(F32).astype(BF16)
            ens = dot(f, pick)
            ybar = jnp.sum(ens, axis=0, keepdims=True) * (1.0 / K)
            anom = ens - ybar
            innov = vals[c, l] - ybar
            for i in range(3):
                sc[i, :, col] = (anom * roots[i, l]).astype(BF16)
                acc[i] += anom * (weights[i, l] * innov)
            return carry

        lax.fori_loop(0, LEV, level, 0)

        def gram_of(i):
            return lax.dot_general(
                sc[i], sc[i], (((1,), (1,)), ((), ())), preferred_element_type=F32
            )

        def vec_of(i):
            return jnp.sum(acc[i].T, axis=0, keepdims=True)

        sent = []
        for side, i, to in ((0, 2, left), (1, 0, right)):
            gram[...] = gram_of(i)
            for b, (p, q) in enumerate(PAIRS):
                gs[c, side, b] = gram[p * 128 : p * 128 + 128, q * 128 : q * 128 + 128]
            vs[c, side] = jnp.broadcast_to(vec_of(i), (8, K))
            for k, (src, dst, sem) in enumerate(((gs, gr, gsem), (vs, vr, vsem))):
                copy = pltpu.make_async_remote_copy(
                    src.at[c, side], dst.at[c, side], sem.at[0, c, side], sem.at[1, c, side],
                    device_id=to, device_id_type=MESH,
                )
                copy.start()
                sent.append(copy)
        gram[...] = gram_of(1)
        vec = vec_of(1)

        def parts(l, carry):
            col = pl.ds(pl.multiple_of(l * RC, RC), RC)
            f = fc[l].astype(F32)
            mean = jnp.sum(f, axis=0, keepdims=True) * (1.0 / K)
            xbar[:, col] = jnp.broadcast_to(mean, (8, RC))
            sc[0, :, col], sc[1, :, col] = halves(f - mean)
            return carry

        for copy in sent:
            copy.wait()
        lax.fori_loop(0, LEV, parts, 0)
        vec = vec + vr[c, 0, 0:1] + vr[c, 1, 0:1]
        for b, (p, q) in enumerate(PAIRS):
            block = gram[p * 128 : p * 128 + 128, q * 128 : q * 128 + 128] + gr[c, 0, b] + gr[c, 1, b]
            gram[p * 128 : p * 128 + 128, q * 128 : q * 128 + 128] = block
            if p != q:
                gram[q * 128 : q * 128 + 128, p * 128 : p * 128 + 128] = block.T
        eye = iota((K, K), 0) == iota((K, K), 1)
        amat = gram[...] + jnp.where(eye, K - 1.0, 0.0)
        scale = jnp.sqrt(jnp.sum(jnp.sum(amat * amat, axis=0, keepdims=True), axis=1, keepdims=True))
        first = amat / scale

        def advance(t):
            high, low = halves(t)
            square = dot3((high, low), (high, low))
            return 2.25 * t + dot3(halves(square), halves(0.25 * t - jnp.where(eye, 1.5, 0.0)))

        tz[1] = jnp.where(eye, 1.5, 0.0) - 0.5 * first
        tz[0] = advance(first)

        def newton(i, carry):
            t, z = tz[0], tz[1]
            tz[1] = 1.5 * z - 0.5 * dot3(halves(t), halves(z))
            tz[0] = advance(t)
            return carry

        lax.fori_loop(0, ITERS - 2, newton, 0)
        z = 1.5 * tz[1] - 0.5 * dot3(halves(tz[0]), halves(tz[1]))
        half = jnp.sum(z * vec, axis=1, keepdims=True)
        wbar = jnp.sum(z * half, axis=0, keepdims=True) / scale
        wh, wl = halves(jnp.sqrt((K - 1.0) / scale) * z + wbar)
        for j in range(LEV // 2):
            cols = slice(256 * j, 256 * j + 256)
            new = dot3((wh, wl), (sc[0, :, cols], sc[1, :, cols])) + xbar[0:1, cols]
            st[2 * j] = new[:, :RC].astype(BF16)
            st[2 * j + 1] = new[:, RC:].astype(BF16)
        return carry

    lax.fori_loop(0, CYCLES, cycle, 0)

    def pack(v, carry):
        rows = []
        for b in range(3):
            both = [st[2 * v + p, 128 * b : 128 * b + 128] for p in range(2)]
            rows.append(dot(together, jnp.concatenate(both, axis=0)).astype(BF16))
        leave[pl.ds(v * 8, 8)] = jnp.concatenate(rows, axis=0).reshape(8, 8, 6, 2, RC)
        return carry

    lax.fori_loop(0, 4, pack, 0)

    keep = local(leave.at[mine], b2.at[:, :, :, cells_of(here)], 0)
    keep.start()
    for ch in range(CHUNKS):
        some = pl.ds(ch * PART, PART)

        def return_plane(s, carry, some=some, ch=ch):
            q2, y2, to = plane_partner(s)
            dst = b2.at[:, some, :, cells_of(here)]
            remote(leave.at[y2 * 8 + q2, :, some], dst, pout.at[ch], to).start()
            return carry

        lax.fori_loop(1, 32, return_plane, 0)
    keep.wait()
    for ch in range(CHUNKS):
        some = pl.ds(ch * PART, PART)
        drain(b2.at[:, some, :, pl.ds(0, 31 * RC)], pout.at[ch, 1])

        def return_z(s, carry, some=some, ch=ch):
            z2, to = z_partner(s)
            remote(b2.at[z2, some], o_ref.at[some, :, own_plane], zout.at[ch], to).start()
            return carry

        lax.fori_loop(1, 8, return_z, 0)
    keep = local(b2.at[z], o_ref.at[:, :, own_plane], 0)
    keep.start()
    for ch in range(CHUNKS):
        some = pl.ds(ch * PART, PART)
        drain(b1.at[pl.ds(0, 7), some], zin.at[ch, 0])
        drain(land.at[pl.ds(0, 31), :, some], pin.at[ch, 0])
        drain(land.at[pl.ds(0, 31), :, some], pout.at[ch, 0])
        drain(b1.at[pl.ds(0, 7), some], zout.at[ch, 0])
        drain(o_ref.at[some, :, pl.ds(0, 7 * PLANE)], zout.at[ch, 1])
    for k in range(2):
        drain(near.at[k, pl.ds(0, 6)], csem.at[k, 0])
    keep.wait()


def per_device(members, courant, obs_value, obs_rinv, obs_cell, obs_count):
    vmem = pltpu.VMEM
    dma = pltpu.SemaphoreType.DMA
    return pl.pallas_call(
        whole_kernel,
        out_shape=jax.ShapeDtypeStruct(members.shape, BF16),
        in_specs=[pl.BlockSpec(memory_space=pl.ANY)] * 6,
        out_specs=pl.BlockSpec(memory_space=pl.ANY),
        scratch_shapes=[
            vmem((8, 6, 2, PLANE), BF16),
            vmem((32, 8, 6, 2, RC), BF16),
            vmem((32, 8, 6, 2, RC), BF16),
            vmem((8, 6, 2, PLANE), BF16),
            vmem((LEV, K, RC), BF16),
            vmem((2, LEV, 1, RC), F32),
            vmem((CYCLES, LEV, 8, RC), F32),
            vmem((LEV, 8, RC), F32),
            vmem((LEV, 8, RC), jnp.int32),
            vmem((LEV, 256), jnp.int32),
            vmem((CYCLES, LEV, 1, RC), F32),
            vmem((LEV, 1, RC), jnp.int32),
            vmem((3, LEV, 1, RC), F32),
            vmem((3, LEV, 1, RC), F32),
            vmem((LEV, K, RC), BF16),
            vmem((3, K, LEV * RC), BF16),
            vmem((3, K, RC), F32),
            vmem((K, K), F32),
            vmem((2, K, K), F32),
            vmem((8, LEV * RC), F32),
            vmem((CYCLES, K, RC), BF16),
            vmem((CYCLES, K, RC), BF16),
            vmem((CYCLES, 2, 6, 128, 128), F32),
            vmem((CYCLES, 2, 6, 128, 128), F32),
            vmem((CYCLES, 2, 8, K), F32),
            vmem((CYCLES, 2, 8, K), F32),
            dma((CHUNKS, 2)),
            dma((CHUNKS, 2)),
            dma((CHUNKS, 2)),
            dma((CHUNKS, 2)),
            dma((2, 2)),
            dma((4,)),
            dma((3,)),
            dma((2, CYCLES)),
            dma((2, CYCLES, 2)),
            dma((2, CYCLES, 2)),
        ],
        compiler_params=pltpu.CompilerParams(
            collective_id=0, has_side_effects=True, vmem_limit_bytes=56 * 2**20
        ),
    )(members, courant.reshape(2, 1, -1), obs_value, obs_rinv, obs_cell, obs_count)


def solution(mesh):
    placed = (P("wide", "layer", None), P("layer", None), P(), P(), P(), P())
    return jax.shard_map(
        per_device, mesh=mesh, in_specs=placed, out_specs=P("wide", "layer", None), check_vma=False
    )
```

```python
import functools

import jax
import jax.numpy as jnp
from jax import lax
from jax.experimental import pallas as pl
from jax.experimental.pallas import tpu as pltpu
from jax.sharding import PartitionSpec as P

K = 384
LEV = 8
RC = 128
ITERS = 5
CYCLES = 2
F32, BF16 = jnp.float32, jnp.bfloat16
MESH = pl.DeviceIdType.MESH
CHUNKS = 3
PART = 6 // CHUNKS
PLANE = 32 * RC
PAIRS = ((0, 0), (0, 1), (0, 2), (1, 1), (1, 2), (2, 2))


def order_in_plane(z, q, y):
    a = (y + z) % 4
    return a * 8 + ((q // 2 + a) % 4) * 2 + q % 2


def device_of(r):
    z, a, b, core = r // 32, (r // 8) % 4, (r // 2) % 4, r % 2
    return z * 8 + ((b - a + 4) % 4) * 2 + core, (a - z + 8) % 4


def dot(a, b):
    return jnp.dot(a, b, preferred_element_type=F32)


def halves(a):
    high = a.astype(BF16)
    return high, (a - high.astype(F32)).astype(BF16)


def dot3(a, b):
    (ah, al), (bh, bl) = a, b
    return dot(ah, bh) + dot(ah, bl) + dot(al, bh)


def iota(shape, dim):
    return lax.broadcasted_iota(jnp.int32, shape, dim)


def whole_kernel(
    mem_ref, cour_ref, val_ref, rinv_ref, cell_ref, count_ref, o_ref,
    b1, land, leave, b2, st, pair, near, tabv, tabr, tabc, tabn, vals, cells, roots, weights,
    fc, sc, acc, gram, tz, xbar, hs, hr, gs, gr, vs, vr,
    zin, pin, pout, zout, csem, tsem, lsem, hsem, gsem, vsem,
):
    w, y = lax.axis_index("wide"), lax.axis_index("layer")
    z, q = w // 8, w % 8
    here = order_in_plane(z, q, y)
    me = z * 32 + here
    mine = y * 8 + q
    left, right = device_of((me + 255) % 256), device_of((me + 1) % 256)

    def z_partner(s):
        z2 = (z + s) % 8
        return z2, (z2 * 8 + q, y)

    def plane_partner(s):
        q2, y2 = (q + s) % 8, (y + s // 8) % 4
        return q2, y2, (z * 8 + q2, y2)

    def cells_of(r, n=RC):
        return pl.ds(pl.multiple_of(r * RC, RC), n)

    def remote(src, dst, sems, to):
        return pltpu.make_async_remote_copy(
            src, dst, sems.at[0], sems.at[1], device_id=to, device_id_type=MESH
        )

    def drain(ref, sem):
        pltpu.make_async_copy(ref, ref, sem).wait()

    def local(src, dst, k):
        return pltpu.make_async_copy(src, dst, lsem.at[k])

    barrier = pltpu.get_barrier_semaphore()

    def greet(device):
        pl.semaphore_signal(barrier, inc=1, device_id=device, device_id_type=MESH)

    def greet_plane(s, carry):
        greet(plane_partner(s)[2])
        return carry

    def greet_z(s, carry):
        greet(z_partner(s)[1])
        return carry

    lax.fori_loop(1, 8, greet_z, 0)
    lax.fori_loop(1, 32, greet_plane, 0)
    greet(left)
    greet(right)
    row8 = pl.ds(pl.multiple_of(me // 8 * 8, 8), 8)
    tables = [
        pltpu.make_async_copy(val_ref.at[:, :, row8], tabv, tsem.at[0]),
        pltpu.make_async_copy(rinv_ref.at[:, row8], tabr, tsem.at[1]),
        pltpu.make_async_copy(cell_ref.at[:, row8], tabc, tsem.at[2]),
        pltpu.make_async_copy(count_ref, tabn, tsem.at[3]),
    ]
    for copy in tables:
        copy.start()
    own_plane = cells_of(z * 32, PLANE)
    keep = local(mem_ref.at[:, :, own_plane], b1.at[z], 0)
    keep.start()
    pl.semaphore_wait(barrier, 40)

    for ch in range(CHUNKS):
        some = pl.ds(ch * PART, PART)

        def send_z(s, carry, some=some, ch=ch):
            z2, to = z_partner(s)
            src = mem_ref.at[some, :, cells_of(z2 * 32, PLANE)]
            remote(src, b1.at[z, some], zin.at[ch], to).start()
            return carry

        lax.fori_loop(1, 8, send_z, 0)

    before_me = (me + 255) % 256
    keeps = [local(cour_ref.at[:, cells_of(me)], pair.at[0, y], 1),
             local(cour_ref.at[:, cells_of(before_me)], pair.at[1, y], 2)]
    for copy in keeps:
        copy.start()

    def send_courant(s, carry):
        y2 = (y + s) % 4
        r = z * 32 + order_in_plane(z, q, y2)
        for k, r2 in enumerate((r, (r + 255) % 256)):
            dst = pair.at[k, y]
            remote(cour_ref.at[:, cells_of(r2)], dst, csem.at[k], (w, y2)).start()
        return carry

    lax.fori_loop(1, 4, send_courant, 0)

    for copy in tables:
        copy.wait()
    mine8 = me % 8
    at8 = iota((8, RC), 0) == mine8
    count = jnp.sum(jnp.where(iota((LEV, 256), 1) == me, tabn[...], 0), axis=1, keepdims=True)
    live = (iota((LEV, RC), 1) < count).astype(F32)
    for l in range(LEV):
        for c in range(CYCLES):
            vals[c, l] = jnp.sum(jnp.where(at8, tabv[c, l], 0.0), axis=0, keepdims=True)
        cell = jnp.sum(jnp.where(at8, tabc[l], 0), axis=0, keepdims=True)
        cells[l] = cell
        rinv = jnp.sum(jnp.where(at8, tabr[l], 0.0), axis=0, keepdims=True)
        for i in range(3):
            ratio = (((i - 1) * RC + cell).astype(F32) - 0.5 * (RC - 1)) * (1.0 / RC)
            weight = rinv * jnp.exp(-(ratio * ratio)) * live[l : l + 1]
            weights[i, l] = weight
            roots[i, l] = jnp.sqrt(weight)
    keep.wait()

    for ch in range(CHUNKS):
        some = pl.ds(ch * PART, PART)
        drain(b1.at[pl.ds(0, 7), some], zin.at[ch, 1])

        def send_plane(s, carry, some=some, ch=ch):
            q2, y2, to = plane_partner(s)
            src = b1.at[:, some, :, cells_of(order_in_plane(z, q2, y2))]
            remote(src, land.at[mine, :, some], pin.at[ch], to).start()
            return carry

        lax.fori_loop(1, 32, send_plane, 0)
    keep = local(b1.at[:, :, :, cells_of(here)], land.at[mine], 0)
    keep.start()
    for copy in keeps:
        copy.wait()
    for k in range(2):
        drain(pair.at[k, pl.ds(0, 3)], csem.at[k, 1])
        for l in range(LEV):
            near[k, l] = pair[k, l // 2, l % 2 : l % 2 + 1]
    keep.wait()
    for ch in range(CHUNKS):
        drain(land.at[pl.ds(0, 31), :, pl.ds(ch * PART, PART)], pin.at[ch, 1])

    out, col = iota((256, 256), 0), iota((256, 256), 1)
    apart = (col == (out % 128) * 2 + out // 128).astype(F32).astype(BF16)
    together = (out == (col % 128) * 2 + col // 128).astype(F32).astype(BF16)

    def unpack(v, carry):
        rows = land[pl.ds(v * 8, 8)].reshape(2 * K, RC)
        for b in range(3):
            both = dot(apart, rows[256 * b : 256 * b + 256]).astype(BF16)
            st[2 * v, 128 * b : 128 * b + 128] = both[:128]
            st[2 * v + 1, 128 * b : 128 * b + 128] = both[128:]
        return carry

    lax.fori_loop(0, 4, unpack, 0)
    lane = iota((K, RC), 1)
    last = lane == RC - 1

    def shifted(u, before):
        return pltpu.roll(jnp.where(last, before, u), 1, axis=1)

    def cycle(c, carry):
        def edge(l, total):
            src, dst = iota((RC, RC), 0), iota((RC, RC), 1)
            pick = (src - (RC - 2) == dst - 2 * l) & (src >= RC - 2)
            return total + dot(st[l], pick.astype(F32).astype(BF16))

        hs[c] = lax.fori_loop(0, LEV, edge, jnp.zeros((K, RC), F32)).astype(BF16)
        halo = pltpu.make_async_remote_copy(
            hs.at[c], hr.at[c], hsem.at[0, c], hsem.at[1, c], device_id=right, device_id_type=MESH
        )
        halo.start()
        halo.wait()
        acc[...] = jnp.zeros_like(acc)

        def level(l, carry):
            col = pl.ds(pl.multiple_of(l * RC, RC), RC)
            own = near[0, l]
            prior = near[1, l]
            before = pltpu.roll(hr[c].astype(F32), RC - 2 - 2 * l, axis=1)
            u = st[l].astype(F32)
            u1 = u - own * (u - shifted(u, before))
            before1 = before - prior * (before - pltpu.roll(before, 1, axis=1))
            f = (u1 - own * (u1 - shifted(u1, before1))).astype(BF16)
            fc[l] = f
            pick = (iota((RC, RC), 0) == cells[l]).astype(F32).astype(BF16)
            ens = dot(f, pick)
            ybar = jnp.sum(ens, axis=0, keepdims=True) * (1.0 / K)
            anom = ens - ybar
            innov = vals[c, l] - ybar
            for i in range(3):
                sc[i, :, col] = (anom * roots[i, l]).astype(BF16)
                acc[i] += anom * (weights[i, l] * innov)
            return carry

        lax.fori_loop(0, LEV, level, 0)

        def gram_of(i):
            return lax.dot_general(
                sc[i], sc[i], (((1,), (1,)), ((), ())), preferred_element_type=F32
            )

        def vec_of(i):
            return jnp.sum(acc[i].T, axis=0, keepdims=True)

        eye = iota((K, K), 0) == iota((K, K), 1)
        eye128 = iota((128, 128), 0) == iota((128, 128), 1)
        sent = []
        for side, i, to in ((0, 2, left), (1, 0, right)):
            gram[...] = gram_of(i)
            for b, (p, q) in enumerate(PAIRS):
                block = gram[p * 128 : p * 128 + 128, q * 128 : q * 128 + 128]
                gs[c, side, b] = (jnp.where(eye128, 0.0, block) if p == q else block).astype(BF16)
            diag = jnp.sum(jnp.where(eye, gram[...], 0.0), axis=0, keepdims=True)
            vs[c, side] = jnp.where(iota((8, K), 0) == 0, vec_of(i), diag)
            for k, (src, dst, sem) in enumerate(((gs, gr, gsem), (vs, vr, vsem))):
                copy = pltpu.make_async_remote_copy(
                    src.at[c, side], dst.at[c, side], sem.at[0, c, side], sem.at[1, c, side],
                    device_id=to, device_id_type=MESH,
                )
                copy.start()
                sent.append(copy)
        gram[...] = gram_of(1)
        vec = vec_of(1)

        def parts(l, carry):
            col = pl.ds(pl.multiple_of(l * RC, RC), RC)
            f = fc[l].astype(F32)
            mean = jnp.sum(f, axis=0, keepdims=True) * (1.0 / K)
            xbar[:, col] = jnp.broadcast_to(mean, (8, RC))
            sc[0, :, col], sc[1, :, col] = halves(f - mean)
            return carry

        for copy in sent:
            copy.wait()
        lax.fori_loop(0, LEV, parts, 0)
        both = vr[c, 0] + vr[c, 1]
        vec, diag = vec + both[0:1], both[1:2]
        for b, (p, q) in enumerate(PAIRS):
            block = gram[p * 128 : p * 128 + 128, q * 128 : q * 128 + 128] + (
                gr[c, 0, b].astype(F32) + gr[c, 1, b].astype(F32)
            )
            gram[p * 128 : p * 128 + 128, q * 128 : q * 128 + 128] = block
            if p != q:
                gram[q * 128 : q * 128 + 128, p * 128 : p * 128 + 128] = block.T
        amat = gram[...] + jnp.where(eye, diag + (K - 1.0), 0.0)
        scale = jnp.sqrt(jnp.sum(jnp.sum(amat * amat, axis=0, keepdims=True), axis=1, keepdims=True))
        first = amat / scale

        def advance(t):
            high, low = halves(t)
            square = dot3((high, low), (high, low))
            return 2.25 * t + dot3(halves(square), halves(0.25 * t - jnp.where(eye, 1.5, 0.0)))

        tz[1] = jnp.where(eye, 1.5, 0.0) - 0.5 * first
        tz[0] = advance(first)

        def newton(i, carry):
            t, z = tz[0], tz[1]
            tz[1] = 1.5 * z - 0.5 * dot3(halves(t), halves(z))
            tz[0] = advance(t)
            return carry

        lax.fori_loop(0, ITERS - 2, newton, 0)
        z = 1.5 * tz[1] - 0.5 * dot3(halves(tz[0]), halves(tz[1]))
        half = jnp.sum(z * vec, axis=1, keepdims=True)
        wbar = jnp.sum(z * half, axis=0, keepdims=True) / scale
        wh, wl = halves(jnp.sqrt((K - 1.0) / scale) * z + wbar)
        for j in range(LEV // 2):
            cols = slice(256 * j, 256 * j + 256)
            new = dot3((wh, wl), (sc[0, :, cols], sc[1, :, cols])) + xbar[0:1, cols]
            st[2 * j] = new[:, :RC].astype(BF16)
            st[2 * j + 1] = new[:, RC:].astype(BF16)
        return carry

    lax.fori_loop(0, CYCLES, cycle, 0)

    def pack(v, carry):
        rows = []
        for b in range(3):
            both = [st[2 * v + p, 128 * b : 128 * b + 128] for p in range(2)]
            rows.append(dot(together, jnp.concatenate(both, axis=0)).astype(BF16))
        leave[pl.ds(v * 8, 8)] = jnp.concatenate(rows, axis=0).reshape(8, 8, 6, 2, RC)
        return carry

    lax.fori_loop(0, 4, pack, 0)

    keep = local(leave.at[mine], b2.at[:, :, :, cells_of(here)], 0)
    keep.start()
    for ch in range(CHUNKS):
        some = pl.ds(ch * PART, PART)

        def return_plane(s, carry, some=some, ch=ch):
            q2, y2, to = plane_partner(s)
            dst = b2.at[:, some, :, cells_of(here)]
            remote(leave.at[y2 * 8 + q2, :, some], dst, pout.at[ch], to).start()
            return carry

        lax.fori_loop(1, 32, return_plane, 0)
    keep.wait()
    for ch in range(CHUNKS):
        some = pl.ds(ch * PART, PART)
        drain(b2.at[:, some, :, pl.ds(0, 31 * RC)], pout.at[ch, 1])

        def return_z(s, carry, some=some, ch=ch):
            z2, to = z_partner(s)
            remote(b2.at[z2, some], o_ref.at[some, :, own_plane], zout.at[ch], to).start()
            return carry

        lax.fori_loop(1, 8, return_z, 0)
    keep = local(b2.at[z], o_ref.at[:, :, own_plane], 0)
    keep.start()
    for ch in range(CHUNKS):
        some = pl.ds(ch * PART, PART)
        drain(b1.at[pl.ds(0, 7), some], zin.at[ch, 0])
        drain(land.at[pl.ds(0, 31), :, some], pin.at[ch, 0])
        drain(land.at[pl.ds(0, 31), :, some], pout.at[ch, 0])
        drain(b1.at[pl.ds(0, 7), some], zout.at[ch, 0])
        drain(o_ref.at[some, :, pl.ds(0, 7 * PLANE)], zout.at[ch, 1])
    for k in range(2):
        drain(pair.at[k, pl.ds(0, 3)], csem.at[k, 0])
    keep.wait()


def per_device(members, courant, obs_value, obs_rinv, obs_cell, obs_count):
    vmem = pltpu.VMEM
    dma = pltpu.SemaphoreType.DMA
    return pl.pallas_call(
        whole_kernel,
        out_shape=jax.ShapeDtypeStruct(members.shape, BF16),
        in_specs=[pl.BlockSpec(memory_space=pl.ANY)] * 6,
        out_specs=pl.BlockSpec(memory_space=pl.ANY),
        scratch_shapes=[
            vmem((8, 6, 2, PLANE), BF16),
            vmem((32, 8, 6, 2, RC), BF16),
            vmem((32, 8, 6, 2, RC), BF16),
            vmem((8, 6, 2, PLANE), BF16),
            vmem((LEV, K, RC), BF16),
            vmem((2, 4, 2, RC), F32),
            vmem((2, LEV, 1, RC), F32),
            vmem((CYCLES, LEV, 8, RC), F32),
            vmem((LEV, 8, RC), F32),
            vmem((LEV, 8, RC), jnp.int32),
            vmem((LEV, 256), jnp.int32),
            vmem((CYCLES, LEV, 1, RC), F32),
            vmem((LEV, 1, RC), jnp.int32),
            vmem((3, LEV, 1, RC), F32),
            vmem((3, LEV, 1, RC), F32),
            vmem((LEV, K, RC), BF16),
            vmem((3, K, LEV * RC), BF16),
            vmem((3, K, RC), F32),
            vmem((K, K), F32),
            vmem((2, K, K), F32),
            vmem((8, LEV * RC), F32),
            vmem((CYCLES, K, RC), BF16),
            vmem((CYCLES, K, RC), BF16),
            vmem((CYCLES, 2, 6, 128, 128), BF16),
            vmem((CYCLES, 2, 6, 128, 128), BF16),
            vmem((CYCLES, 2, 8, K), F32),
            vmem((CYCLES, 2, 8, K), F32),
            dma((CHUNKS, 2)),
            dma((CHUNKS, 2)),
            dma((CHUNKS, 2)),
            dma((CHUNKS, 2)),
            dma((2, 2)),
            dma((4,)),
            dma((3,)),
            dma((2, CYCLES)),
            dma((2, CYCLES, 2)),
            dma((2, CYCLES, 2)),
        ],
        compiler_params=pltpu.CompilerParams(
            collective_id=0, has_side_effects=True, vmem_limit_bytes=56 * 2**20
        ),
    )(members, courant, obs_value, obs_rinv, obs_cell, obs_count)


def solution(mesh):
    placed = (P("wide", "layer", None), P("layer", None), P(), P(), P(), P())
    return jax.shard_map(
        per_device, mesh=mesh, in_specs=placed, out_specs=P("wide", "layer", None), check_vma=False
    )
```

```python
import functools

import jax
import jax.numpy as jnp
from jax import lax
from jax.experimental import pallas as pl
from jax.experimental.pallas import tpu as pltpu
from jax.sharding import PartitionSpec as P

K = 384
LEV = 8
RC = 128
ITERS = 5
CYCLES = 2
F32, BF16 = jnp.float32, jnp.bfloat16
MESH = pl.DeviceIdType.MESH
CHUNKS = 3
PART = 6 // CHUNKS
PLANE = 32 * RC
PAIRS = ((0, 0), (0, 1), (0, 2), (1, 1), (1, 2), (2, 2))


def order_in_plane(z, q, y):
    a = (y + z) % 4
    return a * 8 + ((q // 2 + a) % 4) * 2 + q % 2


def device_of(r):
    z, a, b, core = r // 32, (r // 8) % 4, (r // 2) % 4, r % 2
    return z * 8 + ((b - a + 4) % 4) * 2 + core, (a - z + 8) % 4


def dot(a, b):
    return jnp.dot(a, b, preferred_element_type=F32)


def halves(a):
    high = a.astype(BF16)
    return high, (a - high.astype(F32)).astype(BF16)


def dot3(a, b):
    (ah, al), (bh, bl) = a, b
    return dot(ah, bh) + dot(ah, bl) + dot(al, bh)


def iota(shape, dim):
    return lax.broadcasted_iota(jnp.int32, shape, dim)


def whole_kernel(
    mem_ref, cour_ref, val_ref, rinv_ref, cell_ref, count_ref, o_ref,
    b1, land, leave, b2, st, pair, near, tabv, tabr, tabc, tabn, vals, cells, roots, weights,
    fc, sc, acc, gram, tz, xbar, hs, hr, gs, gr, vs, vr,
    zin, pin, pout, zout, csem, tsem, lsem, hsem, gsem, vsem,
):
    w, y = lax.axis_index("wide"), lax.axis_index("layer")
    z, q = w // 8, w % 8
    here = order_in_plane(z, q, y)
    me = z * 32 + here
    mine = y * 8 + q
    left, right = device_of((me + 255) % 256), device_of((me + 1) % 256)

    def z_partner(s):
        z2 = (z + s) % 8
        return z2, (z2 * 8 + q, y)

    def plane_partner(s):
        q2, y2 = (q + s) % 8, (y + s // 8) % 4
        return q2, y2, (z * 8 + q2, y2)

    def cells_of(r, n=RC):
        return pl.ds(pl.multiple_of(r * RC, RC), n)

    def remote(src, dst, sems, to):
        return pltpu.make_async_remote_copy(
            src, dst, sems.at[0], sems.at[1], device_id=to, device_id_type=MESH
        )

    def drain(ref, sem):
        pltpu.make_async_copy(ref, ref, sem).wait()

    def local(src, dst, k):
        return pltpu.make_async_copy(src, dst, lsem.at[k])

    barrier = pltpu.get_barrier_semaphore()

    def greet(device):
        pl.semaphore_signal(barrier, inc=1, device_id=device, device_id_type=MESH)

    def greet_plane(s, carry):
        greet(plane_partner(s)[2])
        return carry

    def greet_z(s, carry):
        greet(z_partner(s)[1])
        return carry

    lax.fori_loop(1, 8, greet_z, 0)
    lax.fori_loop(1, 32, greet_plane, 0)
    greet(left)
    greet(right)
    row8 = pl.ds(pl.multiple_of(me // 8 * 8, 8), 8)
    tables = [
        pltpu.make_async_copy(val_ref.at[:, :, row8], tabv, tsem.at[0]),
        pltpu.make_async_copy(rinv_ref.at[:, row8], tabr, tsem.at[1]),
        pltpu.make_async_copy(cell_ref.at[:, row8], tabc, tsem.at[2]),
        pltpu.make_async_copy(count_ref, tabn, tsem.at[3]),
    ]
    for copy in tables:
        copy.start()
    own_plane = cells_of(z * 32, PLANE)
    keep = local(mem_ref.at[:, :, own_plane], b1.at[z], 0)
    keep.start()
    pl.semaphore_wait(barrier, 40)

    for ch in range(CHUNKS):
        some = pl.ds(ch * PART, PART)

        def send_z(s, carry, some=some, ch=ch):
            z2, to = z_partner(s)
            src = mem_ref.at[some, :, cells_of(z2 * 32, PLANE)]
            remote(src, b1.at[z, some], zin.at[ch], to).start()
            return carry

        lax.fori_loop(1, 8, send_z, 0)

    before_me = (me + 255) % 256
    keeps = [local(cour_ref.at[:, cells_of(me)], pair.at[0, y], 1),
             local(cour_ref.at[:, cells_of(before_me)], pair.at[1, y], 2)]
    for copy in keeps:
        copy.start()

    def send_courant(s, carry):
        y2 = (y + s) % 4
        r = z * 32 + order_in_plane(z, q, y2)
        for k, r2 in enumerate((r, (r + 255) % 256)):
            dst = pair.at[k, y]
            remote(cour_ref.at[:, cells_of(r2)], dst, csem.at[k], (w, y2)).start()
        return carry

    lax.fori_loop(1, 4, send_courant, 0)

    for copy in tables:
        copy.wait()
    mine8 = me % 8
    at8 = iota((8, RC), 0) == mine8
    count = jnp.sum(jnp.where(iota((LEV, 256), 1) == me, tabn[...], 0), axis=1, keepdims=True)
    live = (iota((LEV, RC), 1) < count).astype(F32)
    for l in range(LEV):
        for c in range(CYCLES):
            vals[c, l] = jnp.sum(jnp.where(at8, tabv[c, l], 0.0), axis=0, keepdims=True)
        cell = jnp.sum(jnp.where(at8, tabc[l], 0), axis=0, keepdims=True)
        cells[l] = cell
        rinv = jnp.sum(jnp.where(at8, tabr[l], 0.0), axis=0, keepdims=True)
        for i in range(3):
            ratio = (((i - 1) * RC + cell).astype(F32) - 0.5 * (RC - 1)) * (1.0 / RC)
            weight = rinv * jnp.exp(-(ratio * ratio)) * live[l : l + 1]
            weights[i, l] = weight
            roots[i, l] = jnp.sqrt(weight)
    keep.wait()

    for ch in range(CHUNKS):
        some = pl.ds(ch * PART, PART)
        drain(b1.at[pl.ds(0, 7), some], zin.at[ch, 1])

        def send_plane(s, carry, some=some, ch=ch):
            q2, y2, to = plane_partner(s)
            src = b1.at[:, some, :, cells_of(order_in_plane(z, q2, y2))]
            remote(src, land.at[mine, :, some], pin.at[ch], to).start()
            return carry

        lax.fori_loop(1, 32, send_plane, 0)
    keep = local(b1.at[:, :, :, cells_of(here)], land.at[mine], 0)
    keep.start()
    for copy in keeps:
        copy.wait()
    for k in range(2):
        drain(pair.at[k, pl.ds(0, 3)], csem.at[k, 1])
        for l in range(LEV):
            near[k, l] = pair[k, l // 2, l % 2 : l % 2 + 1]
    keep.wait()
    for ch in range(CHUNKS):
        drain(land.at[pl.ds(0, 31), :, pl.ds(ch * PART, PART)], pin.at[ch, 1])

    out, col = iota((256, 256), 0), iota((256, 256), 1)
    apart = (col == (out % 128) * 2 + out // 128).astype(F32).astype(BF16)
    together = (out == (col % 128) * 2 + col // 128).astype(F32).astype(BF16)

    def unpack(v, carry):
        rows = land[pl.ds(v * 8, 8)].reshape(2 * K, RC)
        for b in range(3):
            both = dot(apart, rows[256 * b : 256 * b + 256]).astype(BF16)
            st[2 * v, 128 * b : 128 * b + 128] = both[:128]
            st[2 * v + 1, 128 * b : 128 * b + 128] = both[128:]
        return carry

    lax.fori_loop(0, 4, unpack, 0)
    lane = iota((K, RC), 1)
    last = lane == RC - 1

    def shifted(u, before):
        return pltpu.roll(jnp.where(last, before, u), 1, axis=1)

    def pick_edge(l):
        src, dst = iota((RC, RC), 0), iota((RC, RC), 1)
        return ((src - (RC - 2) == dst - 2 * l) & (src >= RC - 2)).astype(F32).astype(BF16)

    def halo(c):
        return remote(hs.at[c], hr.at[c], hsem.at[c], right)

    def edge(l, total):
        return total + dot(st[l], pick_edge(l))

    hs[0] = lax.fori_loop(0, LEV, edge, jnp.zeros((K, RC), F32)).astype(BF16)
    halo(0).start()

    def cycle(c, carry):
        halo(c).wait()
        acc[...] = jnp.zeros_like(acc)

        def level(l, carry):
            col = pl.ds(pl.multiple_of(l * RC, RC), RC)
            own = near[0, l]
            prior = near[1, l]
            before = pltpu.roll(hr[c].astype(F32), RC - 2 - 2 * l, axis=1)
            u = st[l].astype(F32)
            u1 = u - own * (u - shifted(u, before))
            before1 = before - prior * (before - pltpu.roll(before, 1, axis=1))
            f = (u1 - own * (u1 - shifted(u1, before1))).astype(BF16)
            fc[l] = f
            pick = (iota((RC, RC), 0) == cells[l]).astype(F32).astype(BF16)
            ens = dot(f, pick)
            ybar = jnp.sum(ens, axis=0, keepdims=True) * (1.0 / K)
            anom = ens - ybar
            innov = vals[c, l] - ybar
            for i in range(3):
                sc[i, :, col] = (anom * roots[i, l]).astype(BF16)
                acc[i] += anom * (weights[i, l] * innov)
            return carry

        lax.fori_loop(0, LEV, level, 0)

        def gram_of(i):
            return lax.dot_general(
                sc[i], sc[i], (((1,), (1,)), ((), ())), preferred_element_type=F32
            )

        def vec_of(i):
            return jnp.sum(acc[i].T, axis=0, keepdims=True)

        eye = iota((K, K), 0) == iota((K, K), 1)
        eye128 = iota((128, 128), 0) == iota((128, 128), 1)
        sent = []
        for side, i, to in ((0, 2, left), (1, 0, right)):
            gram[...] = gram_of(i)
            for b, (p, q) in enumerate(PAIRS):
                block = gram[p * 128 : p * 128 + 128, q * 128 : q * 128 + 128]
                gs[c, side, b] = (jnp.where(eye128, 0.0, block) if p == q else block).astype(BF16)
            diag = jnp.sum(jnp.where(eye, gram[...], 0.0), axis=0, keepdims=True)
            vs[c, side] = jnp.where(iota((8, K), 0) == 0, vec_of(i), diag)
            for k, (src, dst, sem) in enumerate(((gs, gr, gsem), (vs, vr, vsem))):
                copy = pltpu.make_async_remote_copy(
                    src.at[c, side], dst.at[c, side], sem.at[0, c, side], sem.at[1, c, side],
                    device_id=to, device_id_type=MESH,
                )
                copy.start()
                sent.append(copy)
        gram[...] = gram_of(1)
        vec = vec_of(1)

        def parts(l, carry):
            high_edge, low_edge, mean_edge = carry
            col = pl.ds(pl.multiple_of(l * RC, RC), RC)
            f = fc[l].astype(F32)
            mean = jnp.sum(f, axis=0, keepdims=True) * (1.0 / K)
            xbar[:, col] = jnp.broadcast_to(mean, (8, RC))
            high, low = halves(f - mean)
            sc[0, :, col], sc[1, :, col] = high, low
            pick = pick_edge(l)
            moved = pltpu.roll(jnp.broadcast_to(mean, (8, RC)), 2 * l + 2, axis=1)
            mean_edge = jnp.where(iota((8, RC), 1) // 2 == l, moved, mean_edge)
            return high_edge + dot(high, pick), low_edge + dot(low, pick), mean_edge

        zero = jnp.zeros((K, RC), F32)
        he, le, mean_edge = lax.fori_loop(
            0, LEV, parts, (zero, zero, jnp.zeros((8, RC), F32))
        )
        for copy in sent:
            copy.wait()
        both = vr[c, 0] + vr[c, 1]
        vec, diag = vec + both[0:1], both[1:2]
        for b, (p, q) in enumerate(PAIRS):
            block = gram[p * 128 : p * 128 + 128, q * 128 : q * 128 + 128] + (
                gr[c, 0, b].astype(F32) + gr[c, 1, b].astype(F32)
            )
            gram[p * 128 : p * 128 + 128, q * 128 : q * 128 + 128] = block
            if p != q:
                gram[q * 128 : q * 128 + 128, p * 128 : p * 128 + 128] = block.T
        amat = gram[...] + jnp.where(eye, diag + (K - 1.0), 0.0)
        scale = jnp.sqrt(jnp.sum(jnp.sum(amat * amat, axis=0, keepdims=True), axis=1, keepdims=True))
        first = amat / scale

        def advance(t, times):
            return 2.25 * t + times(times(t, t), 0.25 * t - jnp.where(eye, 1.5, 0.0))

        def once(a, b):
            return dot(a.astype(BF16), b.astype(BF16))

        def thrice(a, b):
            return dot3(halves(a), halves(b))

        def newton(times):
            t, z = tz[0], tz[1]
            tz[1] = 1.5 * z - 0.5 * times(t, z)
            tz[0] = advance(t, times)

        def newton3(i, carry):
            newton(thrice)
            return carry

        tz[1] = jnp.where(eye, 1.5, 0.0) - 0.5 * first
        tz[0] = advance(first, once)
        newton(once)
        lax.fori_loop(0, ITERS - 3, newton3, 0)
        z = 1.5 * tz[1] - 0.5 * thrice(tz[0], tz[1])
        half = jnp.sum(z * vec, axis=1, keepdims=True)
        wbar = jnp.sum(z * half, axis=0, keepdims=True) / scale
        wh, wl = halves(jnp.sqrt((K - 1.0) / scale) * z + wbar)
        edges = dot3((wh, wl), (he.astype(BF16), le.astype(BF16))) + mean_edge[0:1]
        hs[c + 1] = edges.astype(BF16)
        halo(c + 1).start()
        for j in range(LEV // 2):
            cols = slice(256 * j, 256 * j + 256)
            new = dot3((wh, wl), (sc[0, :, cols], sc[1, :, cols])) + xbar[0:1, cols]
            st[2 * j] = new[:, :RC].astype(BF16)
            st[2 * j + 1] = new[:, RC:].astype(BF16)
        return carry

    lax.fori_loop(0, CYCLES, cycle, 0)

    def pack(v, carry):
        rows = []
        for b in range(3):
            both = [st[2 * v + p, 128 * b : 128 * b + 128] for p in range(2)]
            rows.append(dot(together, jnp.concatenate(both, axis=0)).astype(BF16))
        leave[pl.ds(v * 8, 8)] = jnp.concatenate(rows, axis=0).reshape(8, 8, 6, 2, RC)
        return carry

    lax.fori_loop(0, 4, pack, 0)

    keep = local(leave.at[mine], b2.at[:, :, :, cells_of(here)], 0)
    keep.start()
    for ch in range(CHUNKS):
        some = pl.ds(ch * PART, PART)

        def return_plane(s, carry, some=some, ch=ch):
            q2, y2, to = plane_partner(s)
            dst = b2.at[:, some, :, cells_of(here)]
            remote(leave.at[y2 * 8 + q2, :, some], dst, pout.at[ch], to).start()
            return carry

        lax.fori_loop(1, 32, return_plane, 0)
    keep.wait()
    for ch in range(CHUNKS):
        some = pl.ds(ch * PART, PART)
        drain(b2.at[:, some, :, pl.ds(0, 31 * RC)], pout.at[ch, 1])

        def return_z(s, carry, some=some, ch=ch):
            z2, to = z_partner(s)
            remote(b2.at[z2, some], o_ref.at[some, :, own_plane], zout.at[ch], to).start()
            return carry

        lax.fori_loop(1, 8, return_z, 0)
    keep = local(b2.at[z], o_ref.at[:, :, own_plane], 0)
    keep.start()
    for ch in range(CHUNKS):
        some = pl.ds(ch * PART, PART)
        drain(b1.at[pl.ds(0, 7), some], zin.at[ch, 0])
        drain(land.at[pl.ds(0, 31), :, some], pin.at[ch, 0])
        drain(land.at[pl.ds(0, 31), :, some], pout.at[ch, 0])
        drain(b1.at[pl.ds(0, 7), some], zout.at[ch, 0])
        drain(o_ref.at[some, :, pl.ds(0, 7 * PLANE)], zout.at[ch, 1])
    for k in range(2):
        drain(pair.at[k, pl.ds(0, 3)], csem.at[k, 0])
    halo(CYCLES).wait()
    keep.wait()


def per_device(members, courant, obs_value, obs_rinv, obs_cell, obs_count):
    vmem = pltpu.VMEM
    dma = pltpu.SemaphoreType.DMA
    return pl.pallas_call(
        whole_kernel,
        out_shape=jax.ShapeDtypeStruct(members.shape, BF16),
        in_specs=[pl.BlockSpec(memory_space=pl.ANY)] * 6,
        out_specs=pl.BlockSpec(memory_space=pl.ANY),
        scratch_shapes=[
            vmem((8, 6, 2, PLANE), BF16),
            vmem((32, 8, 6, 2, RC), BF16),
            vmem((32, 8, 6, 2, RC), BF16),
            vmem((8, 6, 2, PLANE), BF16),
            vmem((LEV, K, RC), BF16),
            vmem((2, 4, 2, RC), F32),
            vmem((2, LEV, 1, RC), F32),
            vmem((CYCLES, LEV, 8, RC), F32),
            vmem((LEV, 8, RC), F32),
            vmem((LEV, 8, RC), jnp.int32),
            vmem((LEV, 256), jnp.int32),
            vmem((CYCLES, LEV, 1, RC), F32),
            vmem((LEV, 1, RC), jnp.int32),
            vmem((3, LEV, 1, RC), F32),
            vmem((3, LEV, 1, RC), F32),
            vmem((LEV, K, RC), BF16),
            vmem((3, K, LEV * RC), BF16),
            vmem((3, K, RC), F32),
            vmem((K, K), F32),
            vmem((2, K, K), F32),
            vmem((8, LEV * RC), F32),
            vmem((CYCLES + 1, K, RC), BF16),
            vmem((CYCLES + 1, K, RC), BF16),
            vmem((CYCLES, 2, 6, 128, 128), BF16),
            vmem((CYCLES, 2, 6, 128, 128), BF16),
            vmem((CYCLES, 2, 8, K), F32),
            vmem((CYCLES, 2, 8, K), F32),
            dma((CHUNKS, 2)),
            dma((CHUNKS, 2)),
            dma((CHUNKS, 2)),
            dma((CHUNKS, 2)),
            dma((2, 2)),
            dma((4,)),
            dma((3,)),
            dma((CYCLES + 1, 2)),
            dma((2, CYCLES, 2)),
            dma((2, CYCLES, 2)),
        ],
        compiler_params=pltpu.CompilerParams(
            collective_id=0, has_side_effects=True, vmem_limit_bytes=56 * 2**20
        ),
    )(members, courant, obs_value, obs_rinv, obs_cell, obs_count)


def solution(mesh):
    placed = (P("wide", "layer", None), P("layer", None), P(), P(), P(), P())
    return jax.shard_map(
        per_device, mesh=mesh, in_specs=placed, out_specs=P("wide", "layer", None), check_vma=False
    )
```

```python
import functools

import jax
import jax.numpy as jnp
from jax import lax
from jax.experimental import pallas as pl
from jax.experimental.pallas import tpu as pltpu
from jax.sharding import PartitionSpec as P

K = 384
LEV = 8
RC = 128
ITERS = 5
CYCLES = 2
F32, BF16 = jnp.float32, jnp.bfloat16
MESH = pl.DeviceIdType.MESH
CHUNKS = 6
Z_ORDER = (4, 3, 5, 2, 6, 1, 7)
PART = 6 // CHUNKS
PLANE = 32 * RC
PAIRS = ((0, 0), (0, 1), (0, 2), (1, 1), (1, 2), (2, 2))


def order_in_plane(z, q, y):
    a = (y + z) % 4
    return a * 8 + ((q // 2 + a) % 4) * 2 + q % 2


def device_of(r):
    z, a, b, core = r // 32, (r // 8) % 4, (r // 2) % 4, r % 2
    return z * 8 + ((b - a + 4) % 4) * 2 + core, (a - z + 8) % 4


def dot(a, b):
    return jnp.dot(a, b, preferred_element_type=F32)


def halves(a):
    high = a.astype(BF16)
    return high, (a - high.astype(F32)).astype(BF16)


def dot3(a, b):
    (ah, al), (bh, bl) = a, b
    return dot(jnp.concatenate([ah, ah, al], 1), jnp.concatenate([bh, bl, bh], 0))


def iota(shape, dim):
    return lax.broadcasted_iota(jnp.int32, shape, dim)


def whole_kernel(
    mem_ref, cour_ref, val_ref, rinv_ref, cell_ref, count_ref, o_ref,
    b1, land, leave, b2, st, pair, near, tabv, tabr, tabc, tabn, vals, cells, roots, weights,
    fc, sc, acc, gram, tz, xbar, hs, hr, gs, gr, vs, vr,
    zin, pin, pout, zout, csem, tsem, lsem, hsem, gsem, vsem,
):
    w, y = lax.axis_index("wide"), lax.axis_index("layer")
    z, q = w // 8, w % 8
    here = order_in_plane(z, q, y)
    me = z * 32 + here
    mine = y * 8 + q
    left, right = device_of((me + 255) % 256), device_of((me + 1) % 256)

    def z_partner(s):
        z2 = (z + s) % 8
        return z2, (z2 * 8 + q, y)

    def plane_partner(s):
        s = (s * 13) % 32
        q2, y2 = (q + s) % 8, (y + s // 8) % 4
        return q2, y2, (z * 8 + q2, y2)

    def cells_of(r, n=RC):
        return pl.ds(pl.multiple_of(r * RC, RC), n)

    def remote(src, dst, sems, to):
        return pltpu.make_async_remote_copy(
            src, dst, sems.at[0], sems.at[1], device_id=to, device_id_type=MESH
        )

    def drain(ref, sem):
        pltpu.make_async_copy(ref, ref, sem).wait()

    def local(src, dst, k):
        return pltpu.make_async_copy(src, dst, lsem.at[k])

    barrier = pltpu.get_barrier_semaphore()

    def greet(device):
        pl.semaphore_signal(barrier, inc=1, device_id=device, device_id_type=MESH)

    def greet_plane(s, carry):
        greet(plane_partner(s)[2])
        return carry

    def greet_z(s, carry):
        greet(z_partner(s)[1])
        return carry

    lax.fori_loop(1, 8, greet_z, 0)
    lax.fori_loop(1, 32, greet_plane, 0)
    greet(left)
    greet(right)
    row8 = pl.ds(pl.multiple_of(me // 8 * 8, 8), 8)
    tables = [
        pltpu.make_async_copy(val_ref.at[:, :, row8], tabv, tsem.at[0]),
        pltpu.make_async_copy(rinv_ref.at[:, row8], tabr, tsem.at[1]),
        pltpu.make_async_copy(cell_ref.at[:, row8], tabc, tsem.at[2]),
        pltpu.make_async_copy(count_ref, tabn, tsem.at[3]),
    ]
    for copy in tables:
        copy.start()
    own_plane = cells_of(z * 32, PLANE)
    keep = local(mem_ref.at[:, :, own_plane], b1.at[z], 0)
    keep.start()
    pl.semaphore_wait(barrier, 40)

    for ch in range(CHUNKS):
        some = pl.ds(ch * PART, PART)

        def send_z(s, carry, some=some, ch=ch):
            z2, to = z_partner(s)
            src = mem_ref.at[some, :, cells_of(z2 * 32, PLANE)]
            remote(src, b1.at[z, some], zin.at[ch], to).start()
            return carry

        for s in Z_ORDER:
            send_z(s, 0)

    before_me = (me + 255) % 256
    keeps = [local(cour_ref.at[:, cells_of(me)], pair.at[0, y], 1),
             local(cour_ref.at[:, cells_of(before_me)], pair.at[1, y], 2)]
    for copy in keeps:
        copy.start()

    def send_courant(s, carry):
        y2 = (y + s) % 4
        r = z * 32 + order_in_plane(z, q, y2)
        for k, r2 in enumerate((r, (r + 255) % 256)):
            dst = pair.at[k, y]
            remote(cour_ref.at[:, cells_of(r2)], dst, csem.at[k], (w, y2)).start()
        return carry

    lax.fori_loop(1, 4, send_courant, 0)

    for copy in tables:
        copy.wait()
    mine8 = me % 8
    at8 = iota((8, RC), 0) == mine8
    count = jnp.sum(jnp.where(iota((LEV, 256), 1) == me, tabn[...], 0), axis=1, keepdims=True)
    live = (iota((LEV, RC), 1) < count).astype(F32)
    for l in range(LEV):
        for c in range(CYCLES):
            vals[c, l] = jnp.sum(jnp.where(at8, tabv[c, l], 0.0), axis=0, keepdims=True)
        cell = jnp.sum(jnp.where(at8, tabc[l], 0), axis=0, keepdims=True)
        cells[l] = cell
        rinv = jnp.sum(jnp.where(at8, tabr[l], 0.0), axis=0, keepdims=True)
        for i in range(3):
            ratio = (((i - 1) * RC + cell).astype(F32) - 0.5 * (RC - 1)) * (1.0 / RC)
            weight = rinv * jnp.exp(-(ratio * ratio)) * live[l : l + 1]
            weights[i, l] = weight
            roots[i, l] = jnp.sqrt(weight)
    keep.wait()

    for ch in range(CHUNKS):
        some = pl.ds(ch * PART, PART)
        drain(b1.at[pl.ds(0, 7), some], zin.at[ch, 1])

        def send_plane(s, carry, some=some, ch=ch):
            q2, y2, to = plane_partner(s)
            src = b1.at[:, some, :, cells_of(order_in_plane(z, q2, y2))]
            remote(src, land.at[mine, :, some], pin.at[ch], to).start()
            return carry

        lax.fori_loop(1, 32, send_plane, 0)
    keep = local(b1.at[:, :, :, cells_of(here)], land.at[mine], 0)
    keep.start()
    for copy in keeps:
        copy.wait()
    for k in range(2):
        drain(pair.at[k, pl.ds(0, 3)], csem.at[k, 1])
        for l in range(LEV):
            near[k, l] = pair[k, l // 2, l % 2 : l % 2 + 1]
    keep.wait()
    for ch in range(CHUNKS):
        drain(land.at[pl.ds(0, 31), :, pl.ds(ch * PART, PART)], pin.at[ch, 1])

    out, col = iota((256, 256), 0), iota((256, 256), 1)
    apart = (col == (out % 128) * 2 + out // 128).astype(F32).astype(BF16)
    together = (out == (col % 128) * 2 + col // 128).astype(F32).astype(BF16)

    def unpack(v, carry):
        rows = land[pl.ds(v * 8, 8)].reshape(2 * K, RC)
        for b in range(3):
            both = dot(apart, rows[256 * b : 256 * b + 256]).astype(BF16)
            st[2 * v, 128 * b : 128 * b + 128] = both[:128]
            st[2 * v + 1, 128 * b : 128 * b + 128] = both[128:]
        return carry

    lax.fori_loop(0, 4, unpack, 0)
    lane = iota((K, RC), 1)
    last = lane == RC - 1

    def shifted(u, before):
        return pltpu.roll(jnp.where(last, before, u), 1, axis=1)

    def pick_edge(l):
        src, dst = iota((RC, RC), 0), iota((RC, RC), 1)
        return ((src - (RC - 2) == dst - 2 * l) & (src >= RC - 2)).astype(F32).astype(BF16)

    def halo(c):
        return remote(hs.at[c], hr.at[c], hsem.at[c], right)

    def edge(l, total):
        return total + dot(st[l], pick_edge(l))

    hs[0] = lax.fori_loop(0, LEV, edge, jnp.zeros((K, RC), F32)).astype(BF16)
    halo(0).start()

    def cycle(c, carry):
        halo(c).wait()
        acc[...] = jnp.zeros_like(acc)

        def level(l, carry):
            col = pl.ds(pl.multiple_of(l * RC, RC), RC)
            own = near[0, l]
            prior = near[1, l]
            before = pltpu.roll(hr[c].astype(F32), RC - 2 - 2 * l, axis=1)
            u = st[l].astype(F32)
            u1 = u - own * (u - shifted(u, before))
            before1 = before - prior * (before - pltpu.roll(before, 1, axis=1))
            f = (u1 - own * (u1 - shifted(u1, before1))).astype(BF16)
            fc[l] = f
            pick = (iota((RC, RC), 0) == cells[l]).astype(F32).astype(BF16)
            ens = dot(f, pick)
            ybar = jnp.sum(ens, axis=0, keepdims=True) * (1.0 / K)
            anom = ens - ybar
            innov = vals[c, l] - ybar
            for i in range(3):
                sc[i, :, col] = (anom * roots[i, l]).astype(BF16)
                acc[i] += anom * (weights[i, l] * innov)
            return carry

        lax.fori_loop(0, LEV, level, 0)

        def gram_of(i):
            return lax.dot_general(
                sc[i], sc[i], (((1,), (1,)), ((), ())), preferred_element_type=F32
            )

        def vec_of(i):
            return jnp.sum(acc[i].T, axis=0, keepdims=True)

        eye = iota((K, K), 0) == iota((K, K), 1)
        eye128 = iota((128, 128), 0) == iota((128, 128), 1)
        sent = []
        for side, i, to in ((0, 2, left), (1, 0, right)):
            gram[...] = gram_of(i)
            for b, (p, q) in enumerate(PAIRS):
                block = gram[p * 128 : p * 128 + 128, q * 128 : q * 128 + 128]
                gs[c, side, b] = (jnp.where(eye128, 0.0, block) if p == q else block).astype(BF16)
            diag = jnp.sum(jnp.where(eye, gram[...], 0.0), axis=0, keepdims=True)
            vs[c, side] = jnp.where(iota((8, K), 0) == 0, vec_of(i), diag)
            for k, (src, dst, sem) in enumerate(((gs, gr, gsem), (vs, vr, vsem))):
                copy = pltpu.make_async_remote_copy(
                    src.at[c, side], dst.at[c, side], sem.at[0, c, side], sem.at[1, c, side],
                    device_id=to, device_id_type=MESH,
                )
                copy.start()
                sent.append(copy)
        gram[...] = gram_of(1)
        vec = vec_of(1)

        def parts(l, carry):
            high_edge, low_edge, mean_edge = carry
            col = pl.ds(pl.multiple_of(l * RC, RC), RC)
            f = fc[l].astype(F32)
            mean = jnp.sum(f, axis=0, keepdims=True) * (1.0 / K)
            xbar[:, col] = jnp.broadcast_to(mean, (8, RC))
            high, low = halves(f - mean)
            sc[0, :, col], sc[1, :, col] = high, low
            pick = pick_edge(l)
            moved = pltpu.roll(jnp.broadcast_to(mean, (8, RC)), 2 * l + 2, axis=1)
            mean_edge = jnp.where(iota((8, RC), 1) // 2 == l, moved, mean_edge)
            return high_edge + dot(high, pick), low_edge + dot(low, pick), mean_edge

        zero = jnp.zeros((K, RC), F32)
        he, le, mean_edge = lax.fori_loop(
            0, LEV, parts, (zero, zero, jnp.zeros((8, RC), F32))
        )
        for copy in sent:
            copy.wait()
        both = vr[c, 0] + vr[c, 1]
        vec, diag = vec + both[0:1], both[1:2]
        for b, (p, q) in enumerate(PAIRS):
            block = gram[p * 128 : p * 128 + 128, q * 128 : q * 128 + 128] + (
                gr[c, 0, b].astype(F32) + gr[c, 1, b].astype(F32)
            )
            gram[p * 128 : p * 128 + 128, q * 128 : q * 128 + 128] = block
            if p != q:
                gram[q * 128 : q * 128 + 128, p * 128 : p * 128 + 128] = block.T
        amat = gram[...] + jnp.where(eye, diag + (K - 1.0), 0.0)
        scale = jnp.sqrt(jnp.sum(jnp.sum(amat * amat, axis=0, keepdims=True), axis=1, keepdims=True))
        first = amat / scale

        def advance(t, times):
            return 2.25 * t + times(times(t, t), 0.25 * t - jnp.where(eye, 1.5, 0.0))

        def once(a, b):
            return dot(a.astype(BF16), b.astype(BF16))

        def thrice(a, b):
            return dot3(halves(a), halves(b))

        def newton(times):
            t, z = tz[0], tz[1]
            both = times(t, jnp.concatenate([t, z], axis=1))
            tz[1] = 1.5 * z - 0.5 * both[:, K:]
            tz[0] = 2.25 * t + times(both[:, :K], 0.25 * t - jnp.where(eye, 1.5, 0.0))

        def newton3(i, carry):
            newton(thrice)
            return carry

        tz[1] = jnp.where(eye, 1.5, 0.0) - 0.5 * first
        tz[0] = advance(first, once)
        newton(once)
        lax.fori_loop(0, ITERS - 3, newton3, 0)
        z = 1.5 * tz[1] - 0.5 * thrice(tz[0], tz[1])
        half = jnp.sum(z * vec, axis=1, keepdims=True)
        wbar = jnp.sum(z * half, axis=0, keepdims=True) / scale
        wh, wl = halves(jnp.sqrt((K - 1.0) / scale) * z + wbar)
        edges = dot3((wh, wl), (he.astype(BF16), le.astype(BF16))) + mean_edge[0:1]
        hs[c + 1] = edges.astype(BF16)
        halo(c + 1).start()
        for j in range(LEV // 2):
            cols = slice(256 * j, 256 * j + 256)
            new = dot3((wh, wl), (sc[0, :, cols], sc[1, :, cols])) + xbar[0:1, cols]
            st[2 * j] = new[:, :RC].astype(BF16)
            st[2 * j + 1] = new[:, RC:].astype(BF16)
        return carry

    lax.fori_loop(0, CYCLES, cycle, 0)

    def pack(v, carry):
        rows = []
        for b in range(3):
            both = [st[2 * v + p, 128 * b : 128 * b + 128] for p in range(2)]
            rows.append(dot(together, jnp.concatenate(both, axis=0)).astype(BF16))
        leave[pl.ds(v * 8, 8)] = jnp.concatenate(rows, axis=0).reshape(8, 8, 6, 2, RC)
        return carry

    lax.fori_loop(0, 4, pack, 0)

    keep = local(leave.at[mine], b2.at[:, :, :, cells_of(here)], 0)
    keep.start()
    for ch in range(CHUNKS):
        some = pl.ds(ch * PART, PART)

        def return_plane(s, carry, some=some, ch=ch):
            q2, y2, to = plane_partner(s)
            dst = b2.at[:, some, :, cells_of(here)]
            remote(leave.at[y2 * 8 + q2, :, some], dst, pout.at[ch], to).start()
            return carry

        lax.fori_loop(1, 32, return_plane, 0)
    keep.wait()
    for ch in range(CHUNKS):
        some = pl.ds(ch * PART, PART)
        drain(b2.at[:, some, :, pl.ds(0, 31 * RC)], pout.at[ch, 1])

        def return_z(s, carry, some=some, ch=ch):
            z2, to = z_partner(s)
            remote(b2.at[z2, some], o_ref.at[some, :, own_plane], zout.at[ch], to).start()
            return carry

        for s in Z_ORDER:
            return_z(s, 0)
    keep = local(b2.at[z], o_ref.at[:, :, own_plane], 0)
    keep.start()
    for ch in range(CHUNKS):
        some = pl.ds(ch * PART, PART)
        drain(b1.at[pl.ds(0, 7), some], zin.at[ch, 0])
        drain(land.at[pl.ds(0, 31), :, some], pin.at[ch, 0])
        drain(land.at[pl.ds(0, 31), :, some], pout.at[ch, 0])
        drain(b1.at[pl.ds(0, 7), some], zout.at[ch, 0])
        drain(o_ref.at[some, :, pl.ds(0, 7 * PLANE)], zout.at[ch, 1])
    for k in range(2):
        drain(pair.at[k, pl.ds(0, 3)], csem.at[k, 0])
    halo(CYCLES).wait()
    keep.wait()


def per_device(members, courant, obs_value, obs_rinv, obs_cell, obs_count):
    vmem = pltpu.VMEM
    dma = pltpu.SemaphoreType.DMA
    return pl.pallas_call(
        whole_kernel,
        out_shape=jax.ShapeDtypeStruct(members.shape, BF16),
        in_specs=[pl.BlockSpec(memory_space=pl.ANY)] * 6,
        out_specs=pl.BlockSpec(memory_space=pl.ANY),
        scratch_shapes=[
            vmem((8, 6, 2, PLANE), BF16),
            vmem((32, 8, 6, 2, RC), BF16),
            vmem((32, 8, 6, 2, RC), BF16),
            vmem((8, 6, 2, PLANE), BF16),
            vmem((LEV, K, RC), BF16),
            vmem((2, 4, 2, RC), F32),
            vmem((2, LEV, 1, RC), F32),
            vmem((CYCLES, LEV, 8, RC), F32),
            vmem((LEV, 8, RC), F32),
            vmem((LEV, 8, RC), jnp.int32),
            vmem((LEV, 256), jnp.int32),
            vmem((CYCLES, LEV, 1, RC), F32),
            vmem((LEV, 1, RC), jnp.int32),
            vmem((3, LEV, 1, RC), F32),
            vmem((3, LEV, 1, RC), F32),
            vmem((LEV, K, RC), BF16),
            vmem((3, K, LEV * RC), BF16),
            vmem((3, K, RC), F32),
            vmem((K, K), F32),
            vmem((2, K, K), F32),
            vmem((8, LEV * RC), F32),
            vmem((CYCLES + 1, K, RC), BF16),
            vmem((CYCLES + 1, K, RC), BF16),
            vmem((CYCLES, 2, 6, 128, 128), BF16),
            vmem((CYCLES, 2, 6, 128, 128), BF16),
            vmem((CYCLES, 2, 8, K), F32),
            vmem((CYCLES, 2, 8, K), F32),
            dma((CHUNKS, 2)),
            dma((CHUNKS, 2)),
            dma((CHUNKS, 2)),
            dma((CHUNKS, 2)),
            dma((2, 2)),
            dma((4,)),
            dma((3,)),
            dma((CYCLES + 1, 2)),
            dma((2, CYCLES, 2)),
            dma((2, CYCLES, 2)),
        ],
        compiler_params=pltpu.CompilerParams(
            collective_id=0, has_side_effects=True, vmem_limit_bytes=56 * 2**20
        ),
    )(members, courant, obs_value, obs_rinv, obs_cell, obs_count)


def solution(mesh):
    placed = (P("wide", "layer", None), P("layer", None), P(), P(), P(), P())
    return jax.shard_map(
        per_device, mesh=mesh, in_specs=placed, out_specs=P("wide", "layer", None), check_vma=False
    )
```

```python
import functools

import jax
import jax.numpy as jnp
from jax import lax
from jax.experimental import pallas as pl
from jax.experimental.pallas import tpu as pltpu
from jax.sharding import PartitionSpec as P

K = 384
LEV = 8
RC = 128
ITERS = 5
CYCLES = 2
F32, BF16 = jnp.float32, jnp.bfloat16
MESH = pl.DeviceIdType.MESH
CHUNKS = 6
Z_ORDER = (4, 3, 5, 2, 6, 1, 7)
PART = 6 // CHUNKS
PLANE = 32 * RC
PAIRS = ((0, 0), (0, 1), (0, 2), (1, 1), (1, 2), (2, 2))


def order_in_plane(z, q, y):
    a = (y + z) % 4
    return a * 8 + ((q // 2 + a) % 4) * 2 + q % 2


def device_of(r):
    z, a, b, core = r // 32, (r // 8) % 4, (r // 2) % 4, r % 2
    return z * 8 + ((b - a + 4) % 4) * 2 + core, (a - z + 8) % 4


def dot(a, b):
    return jnp.dot(a, b, preferred_element_type=F32)


def halves(a):
    high = a.astype(BF16)
    return high, (a - high.astype(F32)).astype(BF16)


def dot3(a, b):
    (ah, al), (bh, bl) = a, b
    return dot(jnp.concatenate([ah, ah, al], 1), jnp.concatenate([bh, bl, bh], 0))


def iota(shape, dim):
    return lax.broadcasted_iota(jnp.int32, shape, dim)


def whole_kernel(
    mem_ref, cour_ref, val_ref, rinv_ref, cell_ref, count_ref, o_ref,
    b1, land, leave, b2, st, pair, near, tabv, tabr, tabc, tabn, vals, cells, roots, weights,
    fc, sc, acc, gram, tz, xbar, hs, hr, gs, gr, vs, vr,
    zin, pin, pout, zout, csem, tsem, lsem, hsem, gsem, vsem,
):
    w, y = lax.axis_index("wide"), lax.axis_index("layer")
    z, q = w // 8, w % 8
    here = order_in_plane(z, q, y)
    me = z * 32 + here
    mine = y * 8 + q
    left, right = device_of((me + 255) % 256), device_of((me + 1) % 256)

    def z_partner(s):
        z2 = (z + s) % 8
        return z2, (z2 * 8 + q, y)

    def plane_partner(s):
        s = (s * 13) % 32
        q2, y2 = (q + s) % 8, (y + s // 8) % 4
        return q2, y2, (z * 8 + q2, y2)

    def cells_of(r, n=RC):
        return pl.ds(pl.multiple_of(r * RC, RC), n)

    def remote(src, dst, sems, to):
        return pltpu.make_async_remote_copy(
            src, dst, sems.at[0], sems.at[1], device_id=to, device_id_type=MESH
        )

    def drain(ref, sem):
        pltpu.make_async_copy(ref, ref, sem).wait()

    def local(src, dst, k):
        return pltpu.make_async_copy(src, dst, lsem.at[k])

    barrier = pltpu.get_barrier_semaphore()

    def greet(device):
        pl.semaphore_signal(barrier, inc=1, device_id=device, device_id_type=MESH)

    def greet_plane(s, carry):
        greet(plane_partner(s)[2])
        return carry

    def greet_z(s, carry):
        greet(z_partner(s)[1])
        return carry

    lax.fori_loop(1, 8, greet_z, 0)
    lax.fori_loop(1, 32, greet_plane, 0)
    greet(left)
    greet(right)
    row8 = pl.ds(pl.multiple_of(me // 8 * 8, 8), 8)
    tables = [
        pltpu.make_async_copy(val_ref.at[:, :, row8], tabv, tsem.at[0]),
        pltpu.make_async_copy(rinv_ref.at[:, row8], tabr, tsem.at[1]),
        pltpu.make_async_copy(cell_ref.at[:, row8], tabc, tsem.at[2]),
        pltpu.make_async_copy(count_ref, tabn, tsem.at[3]),
    ]
    for copy in tables:
        copy.start()
    own_plane = cells_of(z * 32, PLANE)
    keep = local(mem_ref.at[:, :, own_plane], b1.at[z], 0)
    keep.start()
    pl.semaphore_wait(barrier, 40)

    for ch in range(CHUNKS):
        some = pl.ds(ch * PART, PART)

        def send_z(s, carry, some=some, ch=ch):
            z2, to = z_partner(s)
            src = mem_ref.at[some, :, cells_of(z2 * 32, PLANE)]
            remote(src, b1.at[z, some], zin.at[ch], to).start()
            return carry

        for s in Z_ORDER:
            send_z(s, 0)

    before_me = (me + 255) % 256
    keeps = [local(cour_ref.at[:, cells_of(me)], pair.at[0, y], 1),
             local(cour_ref.at[:, cells_of(before_me)], pair.at[1, y], 2)]
    for copy in keeps:
        copy.start()

    def send_courant(s, carry):
        y2 = (y + s) % 4
        r = z * 32 + order_in_plane(z, q, y2)
        for k, r2 in enumerate((r, (r + 255) % 256)):
            dst = pair.at[k, y]
            remote(cour_ref.at[:, cells_of(r2)], dst, csem.at[k], (w, y2)).start()
        return carry

    lax.fori_loop(1, 4, send_courant, 0)

    for copy in tables:
        copy.wait()
    mine8 = me % 8
    at8 = iota((8, RC), 0) == mine8
    count = jnp.sum(jnp.where(iota((LEV, 256), 1) == me, tabn[...], 0), axis=1, keepdims=True)
    live = (iota((LEV, RC), 1) < count).astype(F32)
    for l in range(LEV):
        for c in range(CYCLES):
            vals[c, l] = jnp.sum(jnp.where(at8, tabv[c, l], 0.0), axis=0, keepdims=True)
        cell = jnp.sum(jnp.where(at8, tabc[l], 0), axis=0, keepdims=True)
        cells[l] = cell
        rinv = jnp.sum(jnp.where(at8, tabr[l], 0.0), axis=0, keepdims=True)
        for i in range(3):
            ratio = (((i - 1) * RC + cell).astype(F32) - 0.5 * (RC - 1)) * (1.0 / RC)
            weight = rinv * jnp.exp(-(ratio * ratio)) * live[l : l + 1]
            weights[i, l] = weight
            roots[i, l] = jnp.sqrt(weight)
    keep.wait()

    for ch in range(CHUNKS):
        some = pl.ds(ch * PART, PART)
        drain(b1.at[pl.ds(0, 7), some], zin.at[ch, 1])

        def send_plane(s, carry, some=some, ch=ch):
            q2, y2, to = plane_partner(s)
            src = b1.at[:, some, :, cells_of(order_in_plane(z, q2, y2))]
            remote(src, land.at[mine, :, some], pin.at[ch], to).start()
            return carry

        lax.fori_loop(1, 32, send_plane, 0)
    keep = local(b1.at[:, :, :, cells_of(here)], land.at[mine], 0)
    keep.start()
    for copy in keeps:
        copy.wait()
    for k in range(2):
        drain(pair.at[k, pl.ds(0, 3)], csem.at[k, 1])
        for l in range(LEV):
            near[k, l] = pair[k, l // 2, l % 2 : l % 2 + 1]
    keep.wait()
    for ch in range(CHUNKS):
        drain(land.at[pl.ds(0, 31), :, pl.ds(ch * PART, PART)], pin.at[ch, 1])

    out, col = iota((256, 256), 0), iota((256, 256), 1)
    apart = (col == (out % 128) * 2 + out // 128).astype(F32).astype(BF16)
    together = (out == (col % 128) * 2 + col // 128).astype(F32).astype(BF16)

    def unpack(v, carry):
        rows = land[pl.ds(v * 8, 8)].reshape(2 * K, RC)
        for b in range(3):
            both = dot(apart, rows[256 * b : 256 * b + 256]).astype(BF16)
            st[2 * v, 128 * b : 128 * b + 128] = both[:128]
            st[2 * v + 1, 128 * b : 128 * b + 128] = both[128:]
        return carry

    lax.fori_loop(0, 4, unpack, 0)
    lane = iota((K, RC), 1)
    last = lane == RC - 1

    def shifted(u, before):
        return pltpu.roll(jnp.where(last, before, u), 1, axis=1)

    def pick_edge(l):
        src, dst = iota((RC, RC), 0), iota((RC, RC), 1)
        return ((src - (RC - 2) == dst - 2 * l) & (src >= RC - 2)).astype(F32).astype(BF16)

    def halo(c):
        return remote(hs.at[c], hr.at[c], hsem.at[c], right)

    def edge(l, total):
        return total + dot(st[l], pick_edge(l))

    hs[0] = lax.fori_loop(0, LEV, edge, jnp.zeros((K, RC), F32)).astype(BF16)
    halo(0).start()

    def cycle(c, carry):
        halo(c).wait()
        acc[...] = jnp.zeros_like(acc)

        def level(l, carry):
            col = pl.ds(pl.multiple_of(l * RC, RC), RC)
            own = near[0, l]
            prior = near[1, l]
            before = pltpu.roll(hr[c].astype(F32), RC - 2 - 2 * l, axis=1)
            u = st[l].astype(F32)
            u1 = u - own * (u - shifted(u, before))
            before1 = before - prior * (before - pltpu.roll(before, 1, axis=1))
            f = (u1 - own * (u1 - shifted(u1, before1))).astype(BF16)
            fc[l] = f
            pick = (iota((RC, RC), 0) == cells[l]).astype(F32).astype(BF16)
            ens = dot(f, pick)
            ybar = jnp.sum(ens, axis=0, keepdims=True) * (1.0 / K)
            anom = ens - ybar
            innov = vals[c, l] - ybar
            for i in range(3):
                sc[i, :, col] = (anom * roots[i, l]).astype(BF16)
                acc[i] += anom * (weights[i, l] * innov)
            return carry

        lax.fori_loop(0, LEV, level, 0)

        def gram_of(i):
            return lax.dot_general(
                sc[i], sc[i], (((1,), (1,)), ((), ())), preferred_element_type=F32
            )

        def vec_of(i):
            return jnp.sum(acc[i].T, axis=0, keepdims=True)

        eye = iota((K, K), 0) == iota((K, K), 1)
        eye128 = iota((128, 128), 0) == iota((128, 128), 1)
        sent = []
        for side, i, to in ((0, 2, left), (1, 0, right)):
            gram[...] = gram_of(i)
            for b, (p, q) in enumerate(PAIRS):
                block = gram[p * 128 : p * 128 + 128, q * 128 : q * 128 + 128]
                gs[c, side, b] = (jnp.where(eye128, 0.0, block) if p == q else block).astype(BF16)
            diag = jnp.sum(jnp.where(eye, gram[...], 0.0), axis=0, keepdims=True)
            vs[c, side] = jnp.where(iota((8, K), 0) == 0, vec_of(i), diag)
            for k, (src, dst, sem) in enumerate(((gs, gr, gsem), (vs, vr, vsem))):
                copy = pltpu.make_async_remote_copy(
                    src.at[c, side], dst.at[c, side], sem.at[0, c, side], sem.at[1, c, side],
                    device_id=to, device_id_type=MESH,
                )
                copy.start()
                sent.append(copy)
        gram[...] = gram_of(1)
        vec = vec_of(1)

        def parts(l, carry):
            high_edge, low_edge, mean_edge = carry
            col = pl.ds(pl.multiple_of(l * RC, RC), RC)
            f = fc[l].astype(F32)
            mean = jnp.sum(f, axis=0, keepdims=True) * (1.0 / K)
            xbar[:, col] = jnp.broadcast_to(mean, (8, RC))
            high, low = halves(f - mean)
            sc[0, :, col], sc[1, :, col] = high, low
            pick = pick_edge(l)
            moved = pltpu.roll(jnp.broadcast_to(mean, (8, RC)), 2 * l + 2, axis=1)
            mean_edge = jnp.where(iota((8, RC), 1) // 2 == l, moved, mean_edge)
            return high_edge + dot(high, pick), low_edge + dot(low, pick), mean_edge

        zero = jnp.zeros((K, RC), F32)
        he, le, mean_edge = lax.fori_loop(
            0, LEV, parts, (zero, zero, jnp.zeros((8, RC), F32))
        )
        for copy in sent:
            copy.wait()
        both = vr[c, 0] + vr[c, 1]
        vec, diag = vec + both[0:1], both[1:2]
        for b, (p, q) in enumerate(PAIRS):
            block = gram[p * 128 : p * 128 + 128, q * 128 : q * 128 + 128] + (
                gr[c, 0, b].astype(F32) + gr[c, 1, b].astype(F32)
            )
            gram[p * 128 : p * 128 + 128, q * 128 : q * 128 + 128] = block
            if p != q:
                gram[q * 128 : q * 128 + 128, p * 128 : p * 128 + 128] = block.T
        amat = gram[...] + jnp.where(eye, diag + (K - 1.0), 0.0)
        scale = jnp.sqrt(jnp.sum(jnp.sum(amat * amat, axis=0, keepdims=True), axis=1, keepdims=True))
        first = amat / scale

        def advance(t, times):
            return 2.25 * t + times(times(t, t), 0.25 * t - jnp.where(eye, 1.5, 0.0))

        def once(a, b):
            return dot(a.astype(BF16), b.astype(BF16))

        def thrice(a, b):
            return dot3(halves(a), halves(b))

        def newton(times):
            t, z = tz[0], tz[1]
            both = times(t, jnp.concatenate([t, z], axis=1))
            tz[1] = 1.5 * z - 0.5 * both[:, K:]
            tz[0] = 2.25 * t + times(both[:, :K], 0.25 * t - jnp.where(eye, 1.5, 0.0))

        def newton3(i, carry):
            newton(thrice)
            return carry

        tz[1] = jnp.where(eye, 1.5, 0.0) - 0.5 * first
        tz[0] = advance(first, once)
        newton(once)
        newton(once)
        lax.fori_loop(0, ITERS - 4, newton3, 0)
        z = 1.5 * tz[1] - 0.5 * thrice(tz[0], tz[1])
        half = jnp.sum(z * vec, axis=1, keepdims=True)
        wbar = jnp.sum(z * half, axis=0, keepdims=True) / scale
        wh, wl = halves(jnp.sqrt((K - 1.0) / scale) * z + wbar)
        edges = dot3((wh, wl), (he.astype(BF16), le.astype(BF16))) + mean_edge[0:1]
        hs[c + 1] = edges.astype(BF16)
        halo(c + 1).start()
        for j in range(LEV // 2):
            cols = slice(256 * j, 256 * j + 256)
            new = dot3((wh, wl), (sc[0, :, cols], sc[1, :, cols])) + xbar[0:1, cols]
            st[2 * j] = new[:, :RC].astype(BF16)
            st[2 * j + 1] = new[:, RC:].astype(BF16)
        return carry

    lax.fori_loop(0, CYCLES, cycle, 0)

    def pack(v, carry):
        rows = []
        for b in range(3):
            both = [st[2 * v + p, 128 * b : 128 * b + 128] for p in range(2)]
            rows.append(dot(together, jnp.concatenate(both, axis=0)).astype(BF16))
        leave[pl.ds(v * 8, 8)] = jnp.concatenate(rows, axis=0).reshape(8, 8, 6, 2, RC)
        return carry

    lax.fori_loop(0, 4, pack, 0)

    keep = local(leave.at[mine], b2.at[:, :, :, cells_of(here)], 0)
    keep.start()
    for ch in range(CHUNKS):
        some = pl.ds(ch * PART, PART)

        def return_plane(s, carry, some=some, ch=ch):
            q2, y2, to = plane_partner(s)
            dst = b2.at[:, some, :, cells_of(here)]
            remote(leave.at[y2 * 8 + q2, :, some], dst, pout.at[ch], to).start()
            return carry

        lax.fori_loop(1, 32, return_plane, 0)
    keep.wait()
    for ch in range(CHUNKS):
        some = pl.ds(ch * PART, PART)
        drain(b2.at[:, some, :, pl.ds(0, 31 * RC)], pout.at[ch, 1])

        def return_z(s, carry, some=some, ch=ch):
            z2, to = z_partner(s)
            remote(b2.at[z2, some], o_ref.at[some, :, own_plane], zout.at[ch], to).start()
            return carry

        for s in Z_ORDER:
            return_z(s, 0)
    keep = local(b2.at[z], o_ref.at[:, :, own_plane], 0)
    keep.start()
    for ch in range(CHUNKS):
        some = pl.ds(ch * PART, PART)
        drain(b1.at[pl.ds(0, 7), some], zin.at[ch, 0])
        drain(land.at[pl.ds(0, 31), :, some], pin.at[ch, 0])
        drain(land.at[pl.ds(0, 31), :, some], pout.at[ch, 0])
        drain(b1.at[pl.ds(0, 7), some], zout.at[ch, 0])
        drain(o_ref.at[some, :, pl.ds(0, 7 * PLANE)], zout.at[ch, 1])
    for k in range(2):
        drain(pair.at[k, pl.ds(0, 3)], csem.at[k, 0])
    halo(CYCLES).wait()
    keep.wait()


def per_device(members, courant, obs_value, obs_rinv, obs_cell, obs_count):
    vmem = pltpu.VMEM
    dma = pltpu.SemaphoreType.DMA
    return pl.pallas_call(
        whole_kernel,
        out_shape=jax.ShapeDtypeStruct(members.shape, BF16),
        in_specs=[pl.BlockSpec(memory_space=pl.ANY)] * 6,
        out_specs=pl.BlockSpec(memory_space=pl.ANY),
        scratch_shapes=[
            vmem((8, 6, 2, PLANE), BF16),
            vmem((32, 8, 6, 2, RC), BF16),
            vmem((32, 8, 6, 2, RC), BF16),
            vmem((8, 6, 2, PLANE), BF16),
            vmem((LEV, K, RC), BF16),
            vmem((2, 4, 2, RC), F32),
            vmem((2, LEV, 1, RC), F32),
            vmem((CYCLES, LEV, 8, RC), F32),
            vmem((LEV, 8, RC), F32),
            vmem((LEV, 8, RC), jnp.int32),
            vmem((LEV, 256), jnp.int32),
            vmem((CYCLES, LEV, 1, RC), F32),
            vmem((LEV, 1, RC), jnp.int32),
            vmem((3, LEV, 1, RC), F32),
            vmem((3, LEV, 1, RC), F32),
            vmem((LEV, K, RC), BF16),
            vmem((3, K, LEV * RC), BF16),
            vmem((3, K, RC), F32),
            vmem((K, K), F32),
            vmem((2, K, K), F32),
            vmem((8, LEV * RC), F32),
            vmem((CYCLES + 1, K, RC), BF16),
            vmem((CYCLES + 1, K, RC), BF16),
            vmem((CYCLES, 2, 6, 128, 128), BF16),
            vmem((CYCLES, 2, 6, 128, 128), BF16),
            vmem((CYCLES, 2, 8, K), F32),
            vmem((CYCLES, 2, 8, K), F32),
            dma((CHUNKS, 2)),
            dma((CHUNKS, 2)),
            dma((CHUNKS, 2)),
            dma((CHUNKS, 2)),
            dma((2, 2)),
            dma((4,)),
            dma((3,)),
            dma((CYCLES + 1, 2)),
            dma((2, CYCLES, 2)),
            dma((2, CYCLES, 2)),
        ],
        compiler_params=pltpu.CompilerParams(
            collective_id=0, has_side_effects=True, vmem_limit_bytes=56 * 2**20
        ),
    )(members, courant, obs_value, obs_rinv, obs_cell, obs_count)


def solution(mesh):
    placed = (P("wide", "layer", None), P("layer", None), P(), P(), P(), P())
    return jax.shard_map(
        per_device, mesh=mesh, in_specs=placed, out_specs=P("wide", "layer", None), check_vma=False
    )
```

```python
import functools

import jax
import jax.numpy as jnp
from jax import lax
from jax.experimental import pallas as pl
from jax.experimental.pallas import tpu as pltpu
from jax.sharding import PartitionSpec as P

K = 384
LEV = 8
RC = 128
ITERS = 5
CYCLES = 2
F32, BF16 = jnp.float32, jnp.bfloat16
MESH = pl.DeviceIdType.MESH
CHUNKS = 6
Z_ORDER = (4, 3, 5, 2, 6, 1, 7)
PART = 6 // CHUNKS
PLANE = 32 * RC
PAIRS = ((0, 0), (0, 1), (0, 2), (1, 1), (1, 2), (2, 2))


def order_in_plane(z, q, y):
    a = (y + z) % 4
    return a * 8 + ((q // 2 + a) % 4) * 2 + q % 2


def device_of(r):
    z, a, b, core = r // 32, (r // 8) % 4, (r // 2) % 4, r % 2
    return z * 8 + ((b - a + 4) % 4) * 2 + core, (a - z + 8) % 4


def dot(a, b):
    return jnp.dot(a, b, preferred_element_type=F32)


def halves(a):
    high = a.astype(BF16)
    return high, (a - high.astype(F32)).astype(BF16)


def dot3(a, b):
    (ah, al), (bh, bl) = a, b
    return dot(jnp.concatenate([ah, ah, al], 1), jnp.concatenate([bh, bl, bh], 0))


def iota(shape, dim):
    return lax.broadcasted_iota(jnp.int32, shape, dim)


def whole_kernel(
    mem_ref, cour_ref, val_ref, rinv_ref, cell_ref, count_ref, o_ref,
    b1, land, leave, b2, st, pair, near, tabv, tabr, tabc, tabn, vals, cells, roots, weights,
    fc, sc, acc, gram, tz, xbar, hs, hr, gs, gr, vs, vr,
    zin, pin, pout, zout, csem, tsem, lsem, hsem, gsem, vsem,
):
    w, y = lax.axis_index("wide"), lax.axis_index("layer")
    z, q = w // 8, w % 8
    here = order_in_plane(z, q, y)
    me = z * 32 + here
    mine = y * 8 + q
    left, right = device_of((me + 255) % 256), device_of((me + 1) % 256)

    def z_partner(s):
        z2 = (z + s) % 8
        return z2, (z2 * 8 + q, y)

    def plane_partner(s):
        s = (s * 13) % 32
        q2, y2 = (q + s) % 8, (y + s // 8) % 4
        return q2, y2, (z * 8 + q2, y2)

    def cells_of(r, n=RC):
        return pl.ds(pl.multiple_of(r * RC, RC), n)

    def remote(src, dst, sems, to):
        return pltpu.make_async_remote_copy(
            src, dst, sems.at[0], sems.at[1], device_id=to, device_id_type=MESH
        )

    def drain(ref, sem):
        pltpu.make_async_copy(ref, ref, sem).wait()

    def local(src, dst, k):
        return pltpu.make_async_copy(src, dst, lsem.at[k])

    barrier = pltpu.get_barrier_semaphore()

    def greet(device):
        pl.semaphore_signal(barrier, inc=1, device_id=device, device_id_type=MESH)

    def greet_plane(s, carry):
        greet(plane_partner(s)[2])
        return carry

    def greet_z(s, carry):
        greet(z_partner(s)[1])
        return carry

    lax.fori_loop(1, 8, greet_z, 0)
    lax.fori_loop(1, 32, greet_plane, 0)
    greet(left)
    greet(right)
    row8 = pl.ds(pl.multiple_of(me // 8 * 8, 8), 8)
    tables = [
        pltpu.make_async_copy(val_ref.at[:, :, row8], tabv, tsem.at[0]),
        pltpu.make_async_copy(rinv_ref.at[:, row8], tabr, tsem.at[1]),
        pltpu.make_async_copy(cell_ref.at[:, row8], tabc, tsem.at[2]),
        pltpu.make_async_copy(count_ref, tabn, tsem.at[3]),
    ]
    for copy in tables:
        copy.start()
    own_plane = cells_of(z * 32, PLANE)
    keep = local(mem_ref.at[:, :, own_plane], b1.at[z], 0)
    keep.start()
    pl.semaphore_wait(barrier, 40)

    for ch in range(CHUNKS):
        some = pl.ds(ch * PART, PART)

        def send_z(s, carry, some=some, ch=ch):
            z2, to = z_partner(s)
            src = mem_ref.at[some, :, cells_of(z2 * 32, PLANE)]
            remote(src, b1.at[z, some], zin.at[ch], to).start()
            return carry

        for s in Z_ORDER:
            send_z(s, 0)

    before_me = (me + 255) % 256
    keeps = [local(cour_ref.at[:, cells_of(me)], pair.at[0, y], 1),
             local(cour_ref.at[:, cells_of(before_me)], pair.at[1, y], 2)]
    for copy in keeps:
        copy.start()

    def send_courant(s, carry):
        y2 = (y + s) % 4
        r = z * 32 + order_in_plane(z, q, y2)
        for k, r2 in enumerate((r, (r + 255) % 256)):
            dst = pair.at[k, y]
            remote(cour_ref.at[:, cells_of(r2)], dst, csem.at[k], (w, y2)).start()
        return carry

    lax.fori_loop(1, 4, send_courant, 0)

    for copy in tables:
        copy.wait()
    mine8 = me % 8
    at8 = iota((8, RC), 0) == mine8
    count = jnp.sum(jnp.where(iota((LEV, 256), 1) == me, tabn[...], 0), axis=1, keepdims=True)
    live = (iota((LEV, RC), 1) < count).astype(F32)
    for l in range(LEV):
        for c in range(CYCLES):
            vals[c, l] = jnp.sum(jnp.where(at8, tabv[c, l], 0.0), axis=0, keepdims=True)
        cell = jnp.sum(jnp.where(at8, tabc[l], 0), axis=0, keepdims=True)
        cells[l] = cell
        rinv = jnp.sum(jnp.where(at8, tabr[l], 0.0), axis=0, keepdims=True)
        for i in range(3):
            ratio = (((i - 1) * RC + cell).astype(F32) - 0.5 * (RC - 1)) * (1.0 / RC)
            weight = rinv * jnp.exp(-(ratio * ratio)) * live[l : l + 1]
            weights[i, l] = weight
            roots[i, l] = jnp.sqrt(weight)
    keep.wait()

    for ch in range(CHUNKS):
        some = pl.ds(ch * PART, PART)
        drain(b1.at[pl.ds(0, 7), some], zin.at[ch, 1])

        def send_plane(s, carry, some=some, ch=ch):
            q2, y2, to = plane_partner(s)
            src = b1.at[:, some, :, cells_of(order_in_plane(z, q2, y2))]
            remote(src, land.at[mine, :, some], pin.at[ch], to).start()
            return carry

        lax.fori_loop(1, 32, send_plane, 0)
    keep = local(b1.at[:, :, :, cells_of(here)], land.at[mine], 0)
    keep.start()
    for copy in keeps:
        copy.wait()
    for k in range(2):
        drain(pair.at[k, pl.ds(0, 3)], csem.at[k, 1])
        for l in range(LEV):
            near[k, l] = pair[k, l // 2, l % 2 : l % 2 + 1]
    keep.wait()
    for ch in range(CHUNKS):
        drain(land.at[pl.ds(0, 31), :, pl.ds(ch * PART, PART)], pin.at[ch, 1])

    out, col = iota((256, 256), 0), iota((256, 256), 1)
    apart = (col == (out % 128) * 2 + out // 128).astype(F32).astype(BF16)
    together = (out == (col % 128) * 2 + col // 128).astype(F32).astype(BF16)

    def unpack(v, carry):
        rows = land[pl.ds(v * 8, 8)].reshape(2 * K, RC)
        for b in range(3):
            both = dot(apart, rows[256 * b : 256 * b + 256]).astype(BF16)
            st[2 * v, 128 * b : 128 * b + 128] = both[:128]
            st[2 * v + 1, 128 * b : 128 * b + 128] = both[128:]
        return carry

    lax.fori_loop(0, 4, unpack, 0)
    lane = iota((K, RC), 1)
    last = lane == RC - 1

    def shifted(u, before):
        return pltpu.roll(jnp.where(last, before, u), 1, axis=1)

    def pick_edge(l):
        src, dst = iota((RC, RC), 0), iota((RC, RC), 1)
        return ((src - (RC - 2) == dst - 2 * l) & (src >= RC - 2)).astype(F32).astype(BF16)

    def halo(c):
        return remote(hs.at[c], hr.at[c], hsem.at[c], right)

    def edge(l, total):
        return total + dot(st[l], pick_edge(l))

    hs[0] = lax.fori_loop(0, LEV, edge, jnp.zeros((K, RC), F32)).astype(BF16)
    halo(0).start()

    def cycle(c, carry):
        halo(c).wait()
        acc[...] = jnp.zeros_like(acc)

        def level(l, carry):
            col = pl.ds(pl.multiple_of(l * RC, RC), RC)
            own = near[0, l]
            prior = near[1, l]
            before = pltpu.roll(hr[c].astype(F32), RC - 2 - 2 * l, axis=1)
            u = st[l].astype(F32)
            u1 = u - own * (u - shifted(u, before))
            before1 = before - prior * (before - pltpu.roll(before, 1, axis=1))
            f = (u1 - own * (u1 - shifted(u1, before1))).astype(BF16)
            fc[l] = f
            pick = (iota((RC, RC), 0) == cells[l]).astype(F32).astype(BF16)
            ens = dot(f, pick)
            ybar = jnp.sum(ens, axis=0, keepdims=True) * (1.0 / K)
            anom = ens - ybar
            innov = vals[c, l] - ybar
            for i in range(3):
                sc[i, :, col] = (anom * roots[i, l]).astype(BF16)
                acc[i] += anom * (weights[i, l] * innov)
            return carry

        lax.fori_loop(0, LEV, level, 0, unroll=2)

        def gram_of(i):
            return lax.dot_general(
                sc[i], sc[i], (((1,), (1,)), ((), ())), preferred_element_type=F32
            )

        def vec_of(i):
            return jnp.sum(acc[i].T, axis=0, keepdims=True)

        eye = iota((K, K), 0) == iota((K, K), 1)
        eye128 = iota((128, 128), 0) == iota((128, 128), 1)
        sent = []
        for side, i, to in ((0, 2, left), (1, 0, right)):
            gram[...] = gram_of(i)
            for b, (p, q) in enumerate(PAIRS):
                block = gram[p * 128 : p * 128 + 128, q * 128 : q * 128 + 128]
                gs[c, side, b] = (jnp.where(eye128, 0.0, block) if p == q else block).astype(BF16)
            diag = jnp.sum(jnp.where(eye, gram[...], 0.0), axis=0, keepdims=True)
            vs[c, side] = jnp.where(iota((8, K), 0) == 0, vec_of(i), diag)
            for k, (src, dst, sem) in enumerate(((gs, gr, gsem), (vs, vr, vsem))):
                copy = pltpu.make_async_remote_copy(
                    src.at[c, side], dst.at[c, side], sem.at[0, c, side], sem.at[1, c, side],
                    device_id=to, device_id_type=MESH,
                )
                copy.start()
                sent.append(copy)
        gram[...] = gram_of(1)
        vec = vec_of(1)

        def parts(l, carry):
            high_edge, low_edge, mean_edge = carry
            col = pl.ds(pl.multiple_of(l * RC, RC), RC)
            f = fc[l].astype(F32)
            mean = jnp.sum(f, axis=0, keepdims=True) * (1.0 / K)
            xbar[:, col] = jnp.broadcast_to(mean, (8, RC))
            high, low = halves(f - mean)
            sc[0, :, col], sc[1, :, col] = high, low
            pick = pick_edge(l)
            moved = pltpu.roll(jnp.broadcast_to(mean, (8, RC)), 2 * l + 2, axis=1)
            mean_edge = jnp.where(iota((8, RC), 1) // 2 == l, moved, mean_edge)
            return high_edge + dot(high, pick), low_edge + dot(low, pick), mean_edge

        zero = jnp.zeros((K, RC), F32)
        he, le, mean_edge = lax.fori_loop(
            0, LEV, parts, (zero, zero, jnp.zeros((8, RC), F32))
        )
        for copy in sent:
            copy.wait()
        both = vr[c, 0] + vr[c, 1]
        vec, diag = vec + both[0:1], both[1:2]
        for b, (p, q) in enumerate(PAIRS):
            block = gram[p * 128 : p * 128 + 128, q * 128 : q * 128 + 128] + (
                gr[c, 0, b].astype(F32) + gr[c, 1, b].astype(F32)
            )
            gram[p * 128 : p * 128 + 128, q * 128 : q * 128 + 128] = block
            if p != q:
                gram[q * 128 : q * 128 + 128, p * 128 : p * 128 + 128] = block.T
        amat = gram[...] + jnp.where(eye, diag + (K - 1.0), 0.0)
        scale = jnp.sqrt(jnp.sum(jnp.sum(amat * amat, axis=0, keepdims=True), axis=1, keepdims=True))
        first = amat / scale

        def advance(t, times):
            return 2.25 * t + times(times(t, t), 0.25 * t - jnp.where(eye, 1.5, 0.0))

        def once(a, b):
            return dot(a.astype(BF16), b.astype(BF16))

        def thrice(a, b):
            return dot3(halves(a), halves(b))

        def newton(times):
            t, z = tz[0], tz[1]
            both = times(t, jnp.concatenate([t, z], axis=1))
            tz[1] = 1.5 * z - 0.5 * both[:, K:]
            tz[0] = 2.25 * t + times(both[:, :K], 0.25 * t - jnp.where(eye, 1.5, 0.0))

        def newton3(i, carry):
            newton(thrice)
            return carry

        tz[1] = jnp.where(eye, 1.5, 0.0) - 0.5 * first
        tz[0] = advance(first, once)
        newton(once)
        newton(once)
        lax.fori_loop(0, ITERS - 4, newton3, 0)
        z = 1.5 * tz[1] - 0.5 * thrice(tz[0], tz[1])
        half = jnp.sum(z * vec, axis=1, keepdims=True)
        wbar = jnp.sum(z * half, axis=0, keepdims=True) / scale
        wh, wl = halves(jnp.sqrt((K - 1.0) / scale) * z + wbar)
        edges = dot3((wh, wl), (he.astype(BF16), le.astype(BF16))) + mean_edge[0:1]
        hs[c + 1] = edges.astype(BF16)
        halo(c + 1).start()
        for j in range(LEV // 2):
            cols = slice(256 * j, 256 * j + 256)
            new = dot3((wh, wl), (sc[0, :, cols], sc[1, :, cols])) + xbar[0:1, cols]
            st[2 * j] = new[:, :RC].astype(BF16)
            st[2 * j + 1] = new[:, RC:].astype(BF16)
        return carry

    lax.fori_loop(0, CYCLES, cycle, 0)

    def pack(v, carry):
        rows = []
        for b in range(3):
            both = [st[2 * v + p, 128 * b : 128 * b + 128] for p in range(2)]
            rows.append(dot(together, jnp.concatenate(both, axis=0)).astype(BF16))
        leave[pl.ds(v * 8, 8)] = jnp.concatenate(rows, axis=0).reshape(8, 8, 6, 2, RC)
        return carry

    lax.fori_loop(0, 4, pack, 0)

    keep = local(leave.at[mine], b2.at[:, :, :, cells_of(here)], 0)
    keep.start()
    for ch in range(CHUNKS):
        some = pl.ds(ch * PART, PART)

        def return_plane(s, carry, some=some, ch=ch):
            q2, y2, to = plane_partner(s)
            dst = b2.at[:, some, :, cells_of(here)]
            remote(leave.at[y2 * 8 + q2, :, some], dst, pout.at[ch], to).start()
            return carry

        lax.fori_loop(1, 32, return_plane, 0)
    keep.wait()
    for ch in range(CHUNKS):
        some = pl.ds(ch * PART, PART)
        drain(b2.at[:, some, :, pl.ds(0, 31 * RC)], pout.at[ch, 1])

        def return_z(s, carry, some=some, ch=ch):
            z2, to = z_partner(s)
            remote(b2.at[z2, some], o_ref.at[some, :, own_plane], zout.at[ch], to).start()
            return carry

        for s in Z_ORDER:
            return_z(s, 0)
    keep = local(b2.at[z], o_ref.at[:, :, own_plane], 0)
    keep.start()
    for ch in range(CHUNKS):
        some = pl.ds(ch * PART, PART)
        drain(b1.at[pl.ds(0, 7), some], zin.at[ch, 0])
        drain(land.at[pl.ds(0, 31), :, some], pin.at[ch, 0])
        drain(land.at[pl.ds(0, 31), :, some], pout.at[ch, 0])
        drain(b1.at[pl.ds(0, 7), some], zout.at[ch, 0])
        drain(o_ref.at[some, :, pl.ds(0, 7 * PLANE)], zout.at[ch, 1])
    for k in range(2):
        drain(pair.at[k, pl.ds(0, 3)], csem.at[k, 0])
    halo(CYCLES).wait()
    keep.wait()


def per_device(members, courant, obs_value, obs_rinv, obs_cell, obs_count):
    vmem = pltpu.VMEM
    dma = pltpu.SemaphoreType.DMA
    return pl.pallas_call(
        whole_kernel,
        out_shape=jax.ShapeDtypeStruct(members.shape, BF16),
        in_specs=[pl.BlockSpec(memory_space=pl.ANY)] * 6,
        out_specs=pl.BlockSpec(memory_space=pl.ANY),
        scratch_shapes=[
            vmem((8, 6, 2, PLANE), BF16),
            vmem((32, 8, 6, 2, RC), BF16),
            vmem((32, 8, 6, 2, RC), BF16),
            vmem((8, 6, 2, PLANE), BF16),
            vmem((LEV, K, RC), BF16),
            vmem((2, 4, 2, RC), F32),
            vmem((2, LEV, 1, RC), F32),
            vmem((CYCLES, LEV, 8, RC), F32),
            vmem((LEV, 8, RC), F32),
            vmem((LEV, 8, RC), jnp.int32),
            vmem((LEV, 256), jnp.int32),
            vmem((CYCLES, LEV, 1, RC), F32),
            vmem((LEV, 1, RC), jnp.int32),
            vmem((3, LEV, 1, RC), F32),
            vmem((3, LEV, 1, RC), F32),
            vmem((LEV, K, RC), BF16),
            vmem((3, K, LEV * RC), BF16),
            vmem((3, K, RC), F32),
            vmem((K, K), F32),
            vmem((2, K, K), F32),
            vmem((8, LEV * RC), F32),
            vmem((CYCLES + 1, K, RC), BF16),
            vmem((CYCLES + 1, K, RC), BF16),
            vmem((CYCLES, 2, 6, 128, 128), BF16),
            vmem((CYCLES, 2, 6, 128, 128), BF16),
            vmem((CYCLES, 2, 8, K), F32),
            vmem((CYCLES, 2, 8, K), F32),
            dma((CHUNKS, 2)),
            dma((CHUNKS, 2)),
            dma((CHUNKS, 2)),
            dma((CHUNKS, 2)),
            dma((2, 2)),
            dma((4,)),
            dma((3,)),
            dma((CYCLES + 1, 2)),
            dma((2, CYCLES, 2)),
            dma((2, CYCLES, 2)),
        ],
        compiler_params=pltpu.CompilerParams(
            collective_id=0, has_side_effects=True, vmem_limit_bytes=56 * 2**20
        ),
    )(members, courant, obs_value, obs_rinv, obs_cell, obs_count)


def solution(mesh):
    placed = (P("wide", "layer", None), P("layer", None), P(), P(), P(), P())
    return jax.shard_map(
        per_device, mesh=mesh, in_specs=placed, out_specs=P("wide", "layer", None), check_vma=False
    )
```
